32 devices in a mesh: section: 2 (over y), grp: 4 (over z), sta: 4 (over x, core).
Axes of the slice: x: 2, y: 2, z: 4, core: 2. Of those that a mesh axis runs over, the one named last changes fastest.
Arguments:
- records: bfloat16 [128, 4, 3, 16384], P(('section', 'grp', 'sta')), may hold values from -6 to 6
- fir_taps: float32 [64], replicated, may hold values from -0.75 to 0.75
- band_bins: int32 [4, 2], replicated, may hold values from 0 to 2048, as said below
- station_live: int32 [128], P(('section', 'grp', 'sta')), may hold values 0 or 1
- block_live: int32 [16], P(('section', 'grp')), may hold values 0 or 1
Outputs:
- correlations: float32 [2304, 16, 1024], P('sta', ('section', 'grp'))
The draws below stay inside these ranges and needn't reach their ends.
Inputs may be any that keep to these rules, and one draw needn't show every extreme that they name: band_bins[b, 0] < band_bins[b, 1]; each band spans 64 to 256 bins.
All inputs are finite; a program needn't handle non-finite values. No bound on the sum of `station_live` or of `block_live` on one device may be relied on, other than what follows from the above.
Results may differ from the reference program's by a relative error of at most 0.0077.
Values may be sent and summed in bfloat16 or wider, within the bound.
No kernel may reach another device: no remote copies, remote signals or barrier semaphores. Data moves between devices by JAX's collectives and lax.ppermute only.
A program may use at most 64 MiB of HBM per device.

```python
import math
import jax
import jax.numpy as jnp
import numpy as np
from jax import lax

GROUP = 16
BINS = 2048
NT = 4096
DEC = 4
RAW = 16384
TAPS = 64
NBANDS = 4
BAND_MIN = 64
BAND_MAX = 256
SEG = 4
OFFS = 2
LAGS = 1024
GROUPS = 8
STATIONS = 128
BLOCKS = 16


def draw_band_bins(key, part):
    key = jax.random.fold_in(key, 11)
    subkeys = jax.random.split(key, 2)
    widths = jax.random.randint(subkeys[0], (NBANDS,), BAND_MIN, BAND_MAX + 1)
    widths = widths.at[0].set(BAND_MAX).at[NBANDS - 1].set(BAND_MIN)
    headroom = BINS - widths + 1
    starts = jax.random.randint(subkeys[1], (NBANDS,), 0, headroom)
    starts = starts.at[0].set(0).at[NBANDS - 1].set(BINS - BAND_MIN)
    return jnp.stack([starts, starts + widths], axis=1).astype(jnp.int32)


def set_ends(array, rng, smallest, top_value):
    longest = array.shape.index(max(array.shape))
    spots = []
    for shift in (0, 1):
        where = [jax.random.randint(jax.random.fold_in(rng, axis), (), 0, length) for axis, length in enumerate(array.shape)]
        where[longest] = (where[longest] + shift) % array.shape[longest]
        spots.append(tuple(where))
    return array.at[spots[0]].set(smallest).at[spots[1]].set(top_value)


def levels(stream_key, extent, cuts, low, high):
    def one(axis_at, shards_of):
        draws = jax.random.uniform(jax.random.fold_in(jax.random.fold_in(stream_key, 6), axis_at), (shards_of,), jnp.float32, low / len(cuts), high / len(cuts))
        return jnp.repeat(jnp.exp(draws), extent[axis_at] // shards_of).reshape((-1,) + (1,) * (len(extent) - axis_at - 1))

    level = one(*cuts[0])
    for cut in cuts[1:]:
        level = level * one(*cut)
    return level


def noise(own_key, extent, width, reach, cuts=(), kind=jnp.bfloat16):
    loudness = levels(own_key, extent, cuts, -0.22, 0.18) if cuts else 1.0
    entries = jax.random.normal(own_key, extent, jnp.float32) * width * loudness
    return jnp.minimum(jnp.maximum(entries, -reach), reach).astype(kind)


def setup_inputs(seed: int = 0) -> dict:
    keys = jax.random.split(jax.random.key(seed), 6)
    return {
        "records": noise(keys[0], (STATIONS, SEG, 3, RAW), 1.0, 6.0, ((0, 32),)),
        "fir_taps": noise(keys[1], (TAPS,), 0.125, 0.75, (), jnp.float32),
        "band_bins": draw_band_bins(jax.random.fold_in(keys[5], 71), 0),
        "station_live": set_ends((jax.random.randint(keys[3], (STATIONS,), 0, 8) < 7).astype(jnp.int32), jax.random.fold_in(keys[3], 1), 0, 1),
        "block_live": set_ends((jax.random.randint(keys[4], (BLOCKS,), 0, 4) < 3).astype(jnp.int32), jax.random.fold_in(keys[4], 1), 0, 1),
    }


epsilon = 1e-06

def decimate(recorded, fir_taps):
    signal = recorded.astype(jnp.float32)
    leading = signal.shape[:-1]
    lead_frames = TAPS // DEC + 1
    phases = jnp.swapaxes(signal.reshape(leading + (NT, DEC)), -1, -2)
    phases = jnp.pad(phases, [(0, 0)] * (len(leading) + 1) + [(lead_frames, 0)])
    summed = jnp.zeros(leading + (NT,), jnp.float32)
    for shift_back in range(lead_frames):
        tap_index = DEC * shift_back - np.arange(DEC)
        usable = (tap_index >= 0) & (tap_index < TAPS)
        coefficients = jnp.where(jnp.asarray(usable), fir_taps[np.clip(tap_index, 0, TAPS - 1)], 0.0)
        window = phases[..., lead_frames - shift_back:lead_frames - shift_back + NT]
        summed = summed + lax.optimization_barrier(jnp.sum(window * coefficients[:, None], axis=-2))
    return summed.astype(jnp.bfloat16)

def dft_table(starts, block_width):
    samples = jnp.arange(NT, dtype=jnp.int32)[:, None]
    bin_index = starts + jnp.arange(block_width, dtype=jnp.int32)[None, :]
    angles = 2.0 * math.pi / NT * (samples * bin_index % NT).astype(jnp.float32)
    return jnp.concatenate([jnp.cos(angles), -jnp.sin(angles)], axis=1).astype(jnp.bfloat16)

def whiten(real_part, imag_part, band_bins, station_live):
    bin_index = jnp.arange(BINS, dtype=jnp.int32)[None, :]
    inside = ((bin_index >= band_bins[:, 0:1]) & (bin_index < band_bins[:, 1:2])).astype(jnp.float32)
    band_width = (band_bins[:, 1] - band_bins[:, 0]).astype(jnp.float32)
    powers = (real_part * real_part + imag_part * imag_part).reshape(-1, BINS)
    energy = jnp.dot(powers, inside.T, precision=lax.Precision.HIGHEST) / band_width
    gains = jnp.dot(lax.rsqrt(energy + epsilon), inside, precision=lax.Precision.HIGHEST)
    gains = gains.reshape(real_part.shape) * station_live.astype(jnp.float32)[:, None, None, None]
    return jnp.concatenate([real_part * gains, imag_part * gains], axis=2).astype(jnp.bfloat16)

def cross_spectra(local_group, remote_group):
    local_re = local_group[:, :, :3].astype(jnp.float32)
    local_im = local_group[:, :, 3:].astype(jnp.float32)
    remote_re = remote_group[:, :, :3].astype(jnp.float32)
    remote_im = remote_group[:, :, 3:].astype(jnp.float32)
    real_sum = jnp.einsum('isaf,jsbf->iajbf', local_re, remote_re) + jnp.einsum('isaf,jsbf->iajbf', local_im, remote_im)
    imag_sum = jnp.einsum('isaf,jsbf->iajbf', local_im, remote_re) - jnp.einsum('isaf,jsbf->iajbf', local_re, remote_im)
    row_count = local_group.shape[0] * 9 * remote_group.shape[0]
    return jnp.concatenate([real_sum.reshape(row_count, -1), imag_sum.reshape(row_count, -1)], axis=1).astype(jnp.bfloat16)

def lag_table(frequency, parity, starts, block_width):
    lag_index = starts + jnp.arange(block_width, dtype=jnp.int32)[None, :] - LAGS // 2
    angles = 2.0 * math.pi / NT * (frequency[:, None] * lag_index % NT).astype(jnp.float32)
    weight = jnp.where(frequency == 0, 0.5, 1.0) / math.sqrt(BINS)
    values = jnp.where(parity[:, None] == 0, jnp.cos(angles), -jnp.sin(angles)) * weight[:, None]
    return values.astype(jnp.bfloat16)

def reference(records, fir_taps, band_bins, station_live, block_live):
    decimated = decimate(records, fir_taps)
    flattened = decimated.reshape(-1, NT)
    product = jnp.dot(flattened, dft_table(0, BINS), preferred_element_type=jnp.float32)
    out_shape = decimated.shape[:-1] + (BINS,)
    real_part = product[:, :BINS].reshape(out_shape)
    imag_part = product[:, BINS:].reshape(out_shape)
    whitened = whiten(real_part, imag_part, band_bins, station_live)
    groups = whitened.reshape(GROUPS, GROUP, SEG, 6, BINS)
    positions = jnp.arange(2 * BINS, dtype=jnp.int32)
    lag_weights = lag_table(positions % BINS, positions // BINS, 0, LAGS)

    def one_block(block_index):
        row_index = block_index // OFFS
        distance = block_index % OFFS + 1
        remote_index = (row_index - distance) % GROUPS
        local_group = lax.dynamic_index_in_dim(groups, row_index, 0, keepdims=False)
        remote_group = lax.dynamic_index_in_dim(groups, remote_index, 0, keepdims=False)
        spectra = cross_spectra(local_group, remote_group)
        kept = block_live[block_index].astype(jnp.float32)
        return jnp.dot(spectra, lag_weights, preferred_element_type=jnp.float32) * kept
    blocks_out = lax.map(one_block, jnp.arange(BLOCKS, dtype=jnp.int32))
    return jnp.transpose(blocks_out, (1, 0, 2))
```

```python
import functools
import math

import jax
import jax.numpy as jnp
import numpy as np
from jax import lax
from jax.experimental import pallas as pl
from jax.experimental.pallas import tpu as pltpu
from jax.sharding import PartitionSpec as P

BINS = 2048
NT = 4096
DEC = 4
RAW = 16384
TAPS = 64
NBANDS = 4
SLOT = 256
OFFS = 2
LAGS = 1024
HALF = LAGS // 2
RADIX = 16
INNER = NT // RADIX
BIG = BINS // RADIX
FOLD = 256 // RADIX
FRAME = 128
SPAN = DEC * FRAME
LEAD = 256
WINDOW = SPAN + LEAD
PIECES = 4
BLOCKS_IN = NT // FRAME
KEPT = NBANDS * SLOT
EPS = 1e-06

f32 = jnp.float32
bf16 = jnp.bfloat16


def by_tile(table):
    padded = np.pad(table, ((0, 0), (0, -table.shape[1] % 128)))
    return np.ascontiguousarray(
        padded.reshape(table.shape[0], -1, 128).transpose(1, 0, 2)
    )


def joined(ref):
    return jnp.concatenate([ref[i] for i in range(ref.shape[0])], axis=1)


def split_const(table):
    high = table.astype(np.float32).astype(bf16)
    low = (table - high.astype(np.float64)).astype(np.float32).astype(bf16)
    return high, low


def compact_order():
    place = np.arange(SLOT)
    return RADIX * (place % FOLD) + place // FOLD


def spectra_constants():
    inner = np.arange(INNER)
    g = np.arange(BIG)
    angle = 2.0 * np.pi * ((inner[:, None] * g[None, :]) % INNER) / INNER
    cos, sin = np.cos(angle), np.sin(angle)
    table = np.concatenate(
        [np.concatenate([cos, -sin], axis=1), np.concatenate([sin, cos], axis=1)], axis=0
    )
    high, low = split_const(table)
    h = np.arange(RADIX)
    turn = 2.0 * np.pi * (h[:, None] * inner[None, :]) / NT
    twiddle = np.stack([np.cos(turn), -np.sin(turn)]).astype(np.float32)
    place = np.zeros((TAPS, WINDOW), np.float32)
    place[np.arange(TAPS), LEAD - np.arange(TAPS)] = 1.0
    fold = np.zeros((RADIX, BIG, SLOT), np.float32)
    for step in range(RADIX):
        fold[step, np.arange(BIG), FOLD * step + np.arange(BIG) % FOLD] = 1.0
    fold = by_tile(fold.reshape(BINS, SLOT).astype(bf16))
    return np.stack([by_tile(high), by_tile(low)]), twiddle, by_tile(place.astype(bf16)), fold


def lag_constants():
    q = compact_order()[:, None].astype(np.float64)
    n = np.arange(HALF)[None, :] + 0.5
    angle = 2.0 * np.pi * ((q * 2 * n) % (2 * NT)) / (2 * NT)
    base = np.stack([np.cos(angle), np.sin(angle)]) / math.sqrt(BINS)
    block = np.arange(16)[:, None].astype(np.float64)
    turn = 2.0 * np.pi * ((block * SLOT * 2 * n) % (2 * NT)) / (2 * NT)
    shift = np.stack([np.cos(turn), np.sin(turn)])
    return base.astype(np.float32), shift.astype(np.float32)


def real_dft8(d):
    r = math.sqrt(0.5)
    s = [d[b] + d[b + 4] for b in range(4)]
    t = [d[b] - d[b + 4] for b in range(4)]
    s02, s13 = s[0] + s[2], s[1] + s[3]
    t13m, t13p = r * (t[1] - t[3]), r * (t[1] + t[3])
    return [
        (s02 + s13, None),
        (t[0] + t13m, -(t[2] + t13p)),
        (s[0] - s[2], s[3] - s[1]),
        (t[0] - t13m, t[2] - t13p),
        (s02 - s13, None),
    ]


def real_dft16(d):
    even, odd = real_dft8(d[0::2]), real_dft8(d[1::2])
    y = [None] * 16
    y[0] = (even[0][0] + odd[0][0], None)
    y[8] = (even[0][0] - odd[0][0], None)
    y[4] = (even[4][0], -odd[4][0])
    for h in range(1, 4):
        c, s = math.cos(math.pi * h / 8), -math.sin(math.pi * h / 8)
        re, im = odd[h]
        tr, ti = re * c - im * s, re * s + im * c
        y[h] = (even[h][0] + tr, even[h][1] + ti)
        y[8 - h] = (even[h][0] - tr, ti - even[h][1])
    for h in range(9, 16):
        y[h] = (y[16 - h][0], -y[16 - h][1])
    return y


def spectra_kernel(
    x_hbm,
    taps_hbm,
    bands_hbm,
    live_hbm,
    table_hbm,
    twiddle_hbm,
    place_hbm,
    fold_hbm,
    order_hbm,
    sent_ref,
    x_ref,
    taps_ref,
    bands_ref,
    live_ref,
    table_ref,
    twiddle_ref,
    place_ref,
    fold_ref,
    order_ref,
    u_high,
    u_low,
    kept,
    sems,
):
    ch = x_ref.shape[0] * x_ref.shape[1]
    piece = RAW // PIECES
    pairs = [(taps_hbm, taps_ref), (place_hbm, place_ref)]
    for i in range(PIECES):
        lanes = slice(i * piece, (i + 1) * piece)
        pairs.append((x_hbm.at[:, :, lanes], x_ref.at[:, :, lanes]))
    pairs += [
        (twiddle_hbm, twiddle_ref),
        (table_hbm, table_ref),
        (bands_hbm, bands_ref),
        (live_hbm, live_ref),
        (fold_hbm, fold_ref),
        (order_hbm, order_ref),
    ]
    copies = [pltpu.make_async_copy(a, b, sems.at[i]) for i, (a, b) in enumerate(pairs)]
    for copy in copies:
        copy.start()
    copies[0].wait()
    taps = taps_ref[...]
    copies[1].wait()
    taps_high = taps.astype(bf16)
    taps_low = (taps - taps_high.astype(f32)).astype(bf16)

    def toeplitz(part):
        row = jnp.dot(part, joined(place_ref), preferred_element_type=f32)
        return pltpu.roll(
            jnp.broadcast_to(row, (FRAME, WINDOW)), 0, 1, stride=DEC, stride_axis=0
        ).astype(bf16)

    weights = jnp.concatenate([toeplitz(taps_high), toeplitz(taps_low)], axis=0)
    decimated = []
    tail = jnp.zeros((ch, LEAD), bf16)
    for i in range(PIECES):
        copies[2 + i].wait()
        x = x_ref[:, :, i * piece : (i + 1) * piece].reshape(ch, piece)
        x = jnp.concatenate([tail, x], axis=1)
        tail = x[:, piece:]
        windows = [x[:, at : at + WINDOW] for at in range(0, piece, SPAN)]
        both = lax.dot_general(
            jnp.concatenate(windows, axis=0),
            weights,
            (((1,), (1,)), ((), ())),
            preferred_element_type=f32,
        )
        decimated.append((both[:, :FRAME] + both[:, FRAME:]).astype(bf16).astype(f32))
    each = BLOCKS_IN // PIECES
    copies[2 + PIECES].wait()
    for at in range(0, ch, 16):
        d = []
        for b in range(RADIX):
            pair = []
            for frame in (2 * b, 2 * b + 1):
                row = frame % each * ch + at
                pair.append(decimated[frame // each][row : row + 16])
            d.append(jnp.concatenate(pair, axis=1))
        y = real_dft16(d)
        for h in range(RADIX):
            c = twiddle_ref[0, h : h + 1, :]
            sn = twiddle_ref[1, h : h + 1, :]
            yr, yi = y[h]
            if yi is None:
                ur, ui = yr * c, yr * sn
            else:
                ur, ui = yr * c - yi * sn, yr * sn + yi * c
            for k, u in enumerate((ur, ui)):
                where = slice(k * INNER, (k + 1) * INNER)
                top = u.astype(bf16)
                u_high[h * ch + at : h * ch + at + 16, where] = top
                u_low[h * ch + at : h * ch + at + 16, where] = (u - top.astype(f32)).astype(bf16)

    for copy in copies[3 + PIECES :]:
        copy.wait()
    table_high, table_low = joined(table_ref.at[0]), joined(table_ref.at[1])
    spectrum = (
        jnp.dot(u_high[...], table_high, preferred_element_type=f32)
        + jnp.dot(u_low[...], table_high, preferred_element_type=f32)
        + jnp.dot(u_high[...], table_low, preferred_element_type=f32)
    )

    row = lax.broadcasted_iota(jnp.int32, (ch, 1), 0)
    station = row // 12
    live = jnp.zeros((ch, 1), f32)
    station_live = live_ref[...].astype(f32)
    for s_at in range(live_ref.shape[1]):
        live = jnp.where(station == s_at, station_live[:, s_at : s_at + 1], live)
    bands = bands_ref[...]
    edges = [[bands[k : k + 1, b : b + 1] for b in range(NBANDS)] for k in range(2)]

    g = lax.broadcasted_iota(jnp.int32, (1, BIG), 1)
    inside = []
    for h in range(RADIX):
        f = RADIX * g + h
        inside.append(
            [
                ((f >= edges[0][b]) & (f < edges[1][b])).astype(f32)
                for b in range(NBANDS)
            ]
        )
    parts = []
    sums = [jnp.zeros((ch, BIG), f32) for _ in range(NBANDS)]
    for h in range(RADIX):
        re = spectrum[h * ch : (h + 1) * ch, :BIG]
        im = spectrum[h * ch : (h + 1) * ch, BIG:]
        parts.append((re, im))
        power = re * re + im * im
        for b in range(NBANDS):
            sums[b] = sums[b] + power * inside[h][b]
    gains = []
    for b in range(NBANDS):
        width = (edges[1][b] - edges[0][b]).astype(f32)
        energy = jnp.sum(sums[b], axis=1, keepdims=True) / width
        gains.append(lax.rsqrt(energy + EPS) * live)

    for h in range(0, RADIX, 2):
        own = []
        gain = [sum(inside[h + e][b] * gains[b] for b in range(NBANDS)) for e in range(2)]
        for b in range(NBANDS):
            pair = []
            for e in range(2):
                mask = inside[h + e][b]
                for earlier in range(b):
                    mask = mask * (1.0 - inside[h + e][earlier])
                pair.append(mask)
            own.append(jnp.concatenate(pair, axis=1).astype(bf16))
        for k in range(2):
            value = jnp.concatenate([parts[h + e][k] * gain[e] for e in range(2)], axis=1)
            value = value.astype(bf16)
            for b in range(NBANDS):
                at = (2 * b + k) * ch
                kept[at : at + ch, h * BIG : (h + 2) * BIG] = value * own[b]
    compact = jnp.dot(kept[...], joined(fold_ref), preferred_element_type=f32).astype(bf16)
    side = jnp.concatenate([compact[at : at + ch] for at in range(0, 2 * NBANDS * ch, ch)], axis=1)
    order = order_ref[...][:, :ch]
    ordered = jnp.dot(order, side, preferred_element_type=f32).astype(bf16)
    for b in range(NBANDS):
        for k in range(2):
            at = (2 * b + k) * SLOT
            sent_ref[k, :, b * SLOT : (b + 1) * SLOT] = ordered[:, at : at + SLOT]


def spectra(records, fir_taps, bands, station_live):
    ns, nw, nc, _ = records.shape
    x = jnp.transpose(records, (0, 2, 1, 3)).reshape(ns * nc, nw, RAW)
    groups = ns * nc
    padded = -(-groups // 4) * 4
    if padded != groups:
        x = jnp.pad(x, ((0, padded - groups), (0, 0), (0, 0)))
    ch = padded * nw
    hbm = pl.BlockSpec(memory_space=pltpu.HBM)
    operands = (x, fir_taps.reshape(1, TAPS), bands, station_live.reshape(1, ns))
    order = np.zeros((nw * groups, -(-ch // 128) * 128), np.float32)
    for w in range(nw):
        for i in range(groups):
            order[w * groups + i, i * nw + w] = 1.0
    operands += spectra_constants() + (order.astype(bf16),)
    return pl.pallas_call(
        spectra_kernel,
        out_shape=jax.ShapeDtypeStruct((2, nw * groups, KEPT), bf16),
        in_specs=[hbm] * len(operands),
        out_specs=pl.BlockSpec(memory_space=pltpu.VMEM),
        scratch_shapes=[pltpu.VMEM(o.shape, o.dtype) for o in operands]
        + [
            pltpu.VMEM((RADIX * ch, 2 * INNER), bf16),
            pltpu.VMEM((RADIX * ch, 2 * INNER), bf16),
            pltpu.VMEM((2 * NBANDS * ch, BINS), bf16),
            pltpu.SemaphoreType.DMA((len(operands) - 1 + PIECES,)),
        ],
        compiler_params=pltpu.CompilerParams(vmem_limit_bytes=62 * 2**20),
        cost_estimate=pl.CostEstimate(
            flops=3 * 10**9, bytes_accessed=5 * 2**20, transcendentals=0
        ),
        name="spectra",
    )(*operands)


def prepare_kernel(peers, bands_ref, sent_ref, turned_ref):
    _, nw, groups, group_rows, _ = turned_ref.shape
    repeats = group_rows // peers
    local_rows = groups * repeats
    place = lax.broadcasted_iota(jnp.int32, (1, SLOT), 1)
    residue = RADIX * (place % FOLD) + place // FOLD
    for b in range(NBANDS):
        start = bands_ref[0, b]
        f = start + ((residue - start) & (SLOT - 1))
        phase = f.astype(f32) * (math.pi / NT)
        c, sn = jnp.cos(phase), jnp.sin(phase)
        where = slice(b * SLOT, (b + 1) * SLOT)
        re, im = sent_ref[0, :, where].astype(f32), sent_ref[1, :, where].astype(f32)
        for k, value in enumerate((re * c + im * sn, im * c - re * sn)):
            for w in range(nw):
                for group in range(groups):
                    rows = []
                    for i in range(group * repeats, (group + 1) * repeats):
                        at = w * local_rows + i
                        rows.append(jnp.broadcast_to(value[at : at + 1], (peers, SLOT)))
                    turned_ref[k, w, group, :, where] = jnp.concatenate(rows, axis=0).astype(bf16)


def prepare(bands, sent, rows, nw):
    peers = 2 * rows
    fit = [n for n in range(1, rows + 1) if rows % n == 0 and n * peers % 16 == 0]
    repeats = fit[0] if fit else rows
    turned = (2, nw, rows // repeats, repeats * peers, KEPT)
    smem = pl.BlockSpec(memory_space=pltpu.SMEM)
    vmem = pl.BlockSpec(memory_space=pltpu.VMEM)
    return pl.pallas_call(
        functools.partial(prepare_kernel, peers),
        out_shape=jax.ShapeDtypeStruct(turned, bf16),
        in_specs=[smem, vmem],
        out_specs=vmem,
        compiler_params=pltpu.CompilerParams(vmem_limit_bytes=16 * 2**20),
        cost_estimate=pl.CostEstimate(flops=10**7, bytes_accessed=4 * 2**20, transcendentals=0),
        name="prepare",
    )(bands, sent)


def lag_kernel(bands_ref, base_ref, shift_ref, even_ref, odd_ref):
    place = lax.broadcasted_iota(jnp.int32, (SLOT, 1), 0)
    residue = RADIX * (place % FOLD) + place // FOLD
    for b in range(NBANDS):
        start = bands_ref[0, b]
        block = start // SLOT
        first = residue >= start % SLOT
        rows = [
            [shift_ref[k, pl.ds(block + step, 1), :] for step in range(2)] for k in range(2)
        ]
        c = jnp.where(first, rows[0][0], rows[0][1])
        s = jnp.where(first, rows[1][0], rows[1][1])
        weight = jnp.where(first & (residue + block * SLOT == 0), 0.5, 1.0)
        bc, bs = base_ref[0] * weight, base_ref[1] * weight
        even_ref[b * SLOT : (b + 1) * SLOT, :] = (bc * c - bs * s).astype(bf16)
        odd_ref[b * SLOT : (b + 1) * SLOT, :] = (bs * c + bc * s).astype(bf16)


def lag_tables(bands):
    base, shift = lag_constants()
    table = jax.ShapeDtypeStruct((KEPT, HALF), bf16)
    smem = pl.BlockSpec(memory_space=pltpu.SMEM)
    vmem = pl.BlockSpec(memory_space=pltpu.VMEM)
    return pl.pallas_call(
        lag_kernel,
        out_shape=[table, table],
        in_specs=[smem, vmem, vmem],
        out_specs=[vmem, vmem],
        compiler_params=pltpu.CompilerParams(vmem_limit_bytes=16 * 2**20),
        cost_estimate=pl.CostEstimate(flops=10**7, bytes_accessed=4 * 2**20, transcendentals=0),
        name="lag_tables",
    )(bands, base, shift)


def crossed(nw, rows, live, lanes, turned_ref, near_ref, swap_ref, cross_re, cross_im):
    _, _, groups, group_rows, _ = turned_ref.shape
    even_core = lax.rem(lax.axis_index("sta"), 2) == 0
    remote = []
    for k in range(2):
        near, swap = near_ref[k, :, lanes], swap_ref[k, :, lanes]
        by_core = [
            jnp.where(even_core, near, swap).astype(f32) * live,
            jnp.where(even_core, swap, near).astype(f32) * live,
        ]
        remote.append([])
        for w in range(nw):
            span = slice(w * rows, (w + 1) * rows)
            peers = jnp.concatenate([made[span] for made in by_core], axis=0)
            repeats = group_rows // (2 * rows)
            remote[k].append(jnp.concatenate([peers] * repeats, axis=0).astype(bf16))
    for row in range(0, group_rows, 16):
        end = min(row + 16, group_rows)
        there = [
            [remote[k][w][row:end] for w in range(nw)]
            for k in range(2)
        ]
        for group in range(groups):
            re, im = [], []
            for w in range(nw):
                lr = turned_ref[0, w, group, row:end, lanes]
                li = turned_ref[1, w, group, row:end, lanes]
                rr, ri = there[0][w], there[1][w]
                re.append(lr * rr + li * ri)
                im.append(li * rr - lr * ri)
            at = slice(group * group_rows + row, group * group_rows + end)
            cross_re[at, lanes] = (re[0] + re[1]) + (re[2] + re[3])
            cross_im[at, lanes] = (im[0] + im[1]) + (im[2] + im[3])


def mirrored(i, even, odd, value_ref):
    _, peers, _ = value_ref.shape
    backward = 127 - lax.broadcasted_iota(jnp.int32, (peers, 128), 1)
    middle = LAGS // 256
    for tile in range(HALF // 128):
        lanes = slice(tile * 128, (tile + 1) * 128)
        e, o = even[:, lanes], odd[:, lanes]
        after, before = (middle + tile) * 128, (middle - 1 - tile) * 128
        value_ref[i, :, after : after + 128] = e - o
        value_ref[i, :, before : before + 128] = jnp.take_along_axis(e + o, backward, axis=1)


def started(i, value_ref, out_ref, block, distance, sems):
    _, chips, _, _, _ = out_ref.shape
    chip = lax.rem(lax.axis_index("sta") // 2 + chips - distance, chips)
    copy = pltpu.make_async_copy(value_ref.at[i], out_ref.at[i, chip, :, block, :], sems.at[i])
    copy.start()
    return copy


def correlate_kernel(nw, batches, aliased, live_ref, turned_ref, even_ref, odd_ref, *rest):
    units = [unit for batch in batches for unit in batch]
    sources, rest = rest[: 2 * len(units)], rest[2 * len(units) :]
    if aliased:
        rest = rest[1:]
    out_ref, cross_re, cross_im, values, sems = rest
    rows = out_ref.shape[0]
    copies = []
    total = turned_ref.shape[2] * turned_ref.shape[3]
    peers = total // rows
    first = 0
    for batch in batches:
        for at in range(first, first + len(batch)):
            live = live_ref[:, units[at][0] : units[at][0] + 1].astype(f32)
            mine = pl.ds(at * total, total)
            for band in range(NBANDS):
                crossed(
                    nw,
                    rows,
                    live,
                    slice(band * SLOT, (band + 1) * SLOT),
                    turned_ref,
                    *sources[2 * at : 2 * at + 2],
                    cross_re.at[mine],
                    cross_im.at[mine],
                )
        span = slice(first * total, (first + len(batch)) * total)
        even = jnp.dot(cross_re[span, :], even_ref[...], preferred_element_type=f32)
        odd = jnp.dot(cross_im[span, :], odd_ref[...], preferred_element_type=f32)
        for at in range(first, first + len(batch)):
            block, distance = units[at]
            value_ref = values.at[at]
            for i in range(rows):
                row = (at - first) * total + i * peers
                mirrored(i, even[row : row + peers], odd[row : row + peers], value_ref)
                copies.append(started(i, value_ref, out_ref, block, distance, sems.at[at]))
        first += len(batch)
    for copy in copies:
        copy.wait()


def correlate(block_live, turned, tables, rows, chips, batches, sources, more=()):
    _, nw, groups, group_rows, _ = turned.shape
    total = groups * group_rows
    peers = 2 * rows
    units = sum(len(batch) for batch in batches)
    vmem = pl.BlockSpec(memory_space=pltpu.VMEM)
    output = pl.BlockSpec(memory_space=pl.ANY)
    operands = [block_live, turned, *tables, *sources]
    cross = pltpu.VMEM((units * total, KEPT), bf16)
    return pl.pallas_call(
        functools.partial(correlate_kernel, nw, batches, bool(more)),
        out_shape=jax.ShapeDtypeStruct((rows, chips, peers, OFFS, LAGS), f32),
        in_specs=[vmem] * len(operands) + [output] * len(more),
        out_specs=output,
        scratch_shapes=[
            cross,
            cross,
            pltpu.VMEM((units, rows, peers, LAGS), f32),
            pltpu.SemaphoreType.DMA((units, rows)),
        ],
        input_output_aliases={len(operands): 0} if more else {},
        compiler_params=pltpu.CompilerParams(vmem_limit_bytes=(24 if more else 32) * 2**20),
        cost_estimate=pl.CostEstimate(
            flops=4 * units * total * KEPT * HALF,
            bytes_accessed=8 * 2**20,
            transcendentals=0,
        ),
        name="last_part" if more else "middle_part",
    )(*operands, *more)


def next_group(block):
    axes = ("section", "grp")
    n = lax.axis_size(axes)
    return lax.ppermute(block, axes, [((i - 1) % n, i) for i in range(n)])


def swapped_core(block):
    n = lax.axis_size("sta")
    return lax.ppermute(block, "sta", [(i, i ^ 1) for i in range(n)])


def from_chip(block, distance):
    n = lax.axis_size("sta")
    return lax.ppermute(block, "sta", [(i, (i + 2 * distance) % n) for i in range(n)])


def tied(*values):
    return lax.optimization_barrier(values)


def body(records, fir_taps, band_bins, station_live, block_live):
    chips = lax.axis_size("sta") // 2
    ns, nw, nc, _ = records.shape
    rows = ns * nc
    bands = jnp.transpose(band_bins)
    sent = spectra(records, fir_taps, bands, station_live)
    turned = prepare(bands, sent, rows, nw)
    tables = lag_tables(bands)
    first, turned, *tables = tied(next_group(sent), turned, *tables)
    second = next_group(first)
    held = [first, swapped_core(first)]
    for d in range(1, chips):
        far = from_chip(first, d)
        held += [far, swapped_core(far)]
    far_second = [from_chip(second, d) for d in range(1, chips)]
    held += [second, swapped_core(second)]
    live = block_live.reshape(1, OFFS)
    batches = [[(0, d) for d in range(chips)], [(1, 0)]]
    result = correlate(live, turned, tables, rows, chips, batches, held)
    far_second, result = tied(far_second, result)
    for d in range(1, chips):
        held = [far_second[d - 1], swapped_core(far_second[d - 1])]
        result = correlate(live, turned, tables, rows, chips, [[(1, d)]], held, (result,))
    return result.reshape(-1, OFFS, LAGS)


def solution(mesh):
    in_specs = (
        P(("section", "grp", "sta"), None, None, None),
        P(),
        P(),
        P(("section", "grp", "sta")),
        P(("section", "grp")),
    )
    out_specs = P("sta", ("section", "grp"), None)
    return jax.shard_map(body, mesh=mesh, in_specs=in_specs, out_specs=out_specs, check_vma=False)
```

```python
import functools
import math

import jax
import jax.numpy as jnp
import numpy as np
from jax import lax
from jax.experimental import pallas as pl
from jax.experimental.pallas import tpu as pltpu
from jax.sharding import PartitionSpec as P

BINS = 2048
NT = 4096
DEC = 4
RAW = 16384
TAPS = 64
NBANDS = 4
SLOT = 256
OFFS = 2
LAGS = 1024
HALF = LAGS // 2
RADIX = 16
INNER = NT // RADIX
BIG = BINS // RADIX
FOLD = 256 // RADIX
FRAME = 128
SPAN = DEC * FRAME
LEAD = 256
WINDOW = SPAN + LEAD
PIECES = 4
BLOCKS_IN = NT // FRAME
KEPT = NBANDS * SLOT
EPS = 1e-06

f32 = jnp.float32
bf16 = jnp.bfloat16


def by_tile(table):
    padded = np.pad(table, ((0, 0), (0, -table.shape[1] % 128)))
    return np.ascontiguousarray(
        padded.reshape(table.shape[0], -1, 128).transpose(1, 0, 2)
    )


def joined(ref):
    return jnp.concatenate([ref[i] for i in range(ref.shape[0])], axis=1)


def compact_order():
    place = np.arange(SLOT)
    return RADIX * (place % FOLD) + place // FOLD


def spectra_constants():
    inner = np.arange(INNER)
    g = np.arange(BIG)
    angle = 2.0 * np.pi * ((inner[:, None] * g[None, :]) % INNER) / INNER
    cos, sin = np.cos(angle), np.sin(angle)
    table = np.concatenate(
        [np.concatenate([cos, -sin], axis=1), np.concatenate([sin, cos], axis=1)], axis=0
    )
    h = np.arange(RADIX)
    turn = 2.0 * np.pi * (h[:, None] * inner[None, :]) / NT
    twiddle = np.stack([np.cos(turn), -np.sin(turn)]).astype(np.float32)
    place = np.zeros((TAPS, WINDOW), np.float32)
    place[np.arange(TAPS), LEAD - np.arange(TAPS)] = 1.0
    fold = np.zeros((RADIX, BIG, SLOT), np.float32)
    for step in range(RADIX):
        fold[step, np.arange(BIG), FOLD * step + np.arange(BIG) % FOLD] = 1.0
    fold = by_tile(fold.reshape(BINS, SLOT).astype(bf16))
    return by_tile(table.astype(np.float32).astype(bf16)), twiddle, by_tile(place.astype(bf16)), fold


def lag_constants():
    q = compact_order()[:, None].astype(np.float64)
    n = np.arange(HALF)[None, :] + 0.5
    angle = 2.0 * np.pi * ((q * 2 * n) % (2 * NT)) / (2 * NT)
    base = np.stack([np.cos(angle), np.sin(angle)]) / math.sqrt(BINS)
    block = np.arange(16)[:, None].astype(np.float64)
    turn = 2.0 * np.pi * ((block * SLOT * 2 * n) % (2 * NT)) / (2 * NT)
    shift = np.stack([np.cos(turn), np.sin(turn)])
    return base.astype(np.float32), shift.astype(np.float32)


def real_dft8(d):
    r = math.sqrt(0.5)
    s = [d[b] + d[b + 4] for b in range(4)]
    t = [d[b] - d[b + 4] for b in range(4)]
    s02, s13 = s[0] + s[2], s[1] + s[3]
    t13m, t13p = r * (t[1] - t[3]), r * (t[1] + t[3])
    return [
        (s02 + s13, None),
        (t[0] + t13m, -(t[2] + t13p)),
        (s[0] - s[2], s[3] - s[1]),
        (t[0] - t13m, t[2] - t13p),
        (s02 - s13, None),
    ]


def real_dft16(d):
    even, odd = real_dft8(d[0::2]), real_dft8(d[1::2])
    y = [None] * 16
    y[0] = (even[0][0] + odd[0][0], None)
    y[8] = (even[0][0] - odd[0][0], None)
    y[4] = (even[4][0], -odd[4][0])
    for h in range(1, 4):
        c, s = math.cos(math.pi * h / 8), -math.sin(math.pi * h / 8)
        re, im = odd[h]
        tr, ti = re * c - im * s, re * s + im * c
        y[h] = (even[h][0] + tr, even[h][1] + ti)
        y[8 - h] = (even[h][0] - tr, ti - even[h][1])
    for h in range(9, 16):
        y[h] = (y[16 - h][0], -y[16 - h][1])
    return y


def spectra_kernel(
    x_hbm,
    taps_hbm,
    bands_hbm,
    live_hbm,
    table_hbm,
    twiddle_hbm,
    place_hbm,
    fold_hbm,
    order_hbm,
    sent_ref,
    x_ref,
    taps_ref,
    bands_ref,
    live_ref,
    table_ref,
    twiddle_ref,
    place_ref,
    fold_ref,
    order_ref,
    turned,
    kept,
    sems,
):
    ch = x_ref.shape[0] * x_ref.shape[1]
    piece = RAW // PIECES
    pairs = [(taps_hbm, taps_ref), (place_hbm, place_ref)]
    for i in range(PIECES):
        lanes = slice(i * piece, (i + 1) * piece)
        pairs.append((x_hbm.at[:, :, lanes], x_ref.at[:, :, lanes]))
    pairs += [
        (twiddle_hbm, twiddle_ref),
        (table_hbm, table_ref),
        (bands_hbm, bands_ref),
        (live_hbm, live_ref),
        (fold_hbm, fold_ref),
        (order_hbm, order_ref),
    ]
    copies = [pltpu.make_async_copy(a, b, sems.at[i]) for i, (a, b) in enumerate(pairs)]
    for copy in copies:
        copy.start()
    copies[0].wait()
    taps = taps_ref[...]
    copies[1].wait()
    taps_high = taps.astype(bf16)
    taps_low = (taps - taps_high.astype(f32)).astype(bf16)

    def toeplitz(part):
        row = jnp.dot(part, joined(place_ref), preferred_element_type=f32)
        return pltpu.roll(
            jnp.broadcast_to(row, (FRAME, WINDOW)), 0, 1, stride=DEC, stride_axis=0
        ).astype(bf16)

    weights = jnp.concatenate([toeplitz(taps_high), toeplitz(taps_low)], axis=0)
    decimated = []
    tail = jnp.zeros((ch, LEAD), bf16)
    for i in range(PIECES):
        copies[2 + i].wait()
        x = x_ref[:, :, i * piece : (i + 1) * piece].reshape(ch, piece)
        x = jnp.concatenate([tail, x], axis=1)
        tail = x[:, piece:]
        windows = [x[:, at : at + WINDOW] for at in range(0, piece, SPAN)]
        both = lax.dot_general(
            jnp.concatenate(windows, axis=0),
            weights,
            (((1,), (1,)), ((), ())),
            preferred_element_type=f32,
        )
        decimated.append((both[:, :FRAME] + both[:, FRAME:]).astype(bf16).astype(f32))
    each = BLOCKS_IN // PIECES
    copies[2 + PIECES].wait()
    for at in range(0, ch, 16):
        d = []
        for b in range(RADIX):
            pair = []
            for frame in (2 * b, 2 * b + 1):
                row = frame % each * ch + at
                pair.append(decimated[frame // each][row : row + 16])
            d.append(jnp.concatenate(pair, axis=1))
        y = real_dft16(d)
        for h in range(RADIX):
            c = twiddle_ref[0, h : h + 1, :]
            sn = twiddle_ref[1, h : h + 1, :]
            yr, yi = y[h]
            if yi is None:
                ur, ui = yr * c, yr * sn
            else:
                ur, ui = yr * c - yi * sn, yr * sn + yi * c
            for k, u in enumerate((ur, ui)):
                where = slice(k * INNER, (k + 1) * INNER)
                turned[h * ch + at : h * ch + at + 16, where] = u.astype(bf16)

    for copy in copies[3 + PIECES :]:
        copy.wait()
    spectrum = jnp.dot(turned[...], joined(table_ref), preferred_element_type=f32)

    row = lax.broadcasted_iota(jnp.int32, (ch, 1), 0)
    station = row // 12
    live = jnp.zeros((ch, 1), f32)
    station_live = live_ref[...].astype(f32)
    for s_at in range(live_ref.shape[1]):
        live = jnp.where(station == s_at, station_live[:, s_at : s_at + 1], live)
    bands = bands_ref[...]
    edges = [[bands[k : k + 1, b : b + 1] for b in range(NBANDS)] for k in range(2)]

    g = lax.broadcasted_iota(jnp.int32, (1, BIG), 1)
    inside = []
    for h in range(RADIX):
        f = RADIX * g + h
        inside.append(
            [
                ((f >= edges[0][b]) & (f < edges[1][b])).astype(f32)
                for b in range(NBANDS)
            ]
        )
    parts = []
    sums = [jnp.zeros((ch, BIG), f32) for _ in range(NBANDS)]
    for h in range(RADIX):
        re = spectrum[h * ch : (h + 1) * ch, :BIG]
        im = spectrum[h * ch : (h + 1) * ch, BIG:]
        parts.append((re, im))
        power = re * re + im * im
        for b in range(NBANDS):
            sums[b] = sums[b] + power * inside[h][b]
    gains = []
    for b in range(NBANDS):
        width = (edges[1][b] - edges[0][b]).astype(f32)
        energy = jnp.sum(sums[b], axis=1, keepdims=True) / width
        gains.append(lax.rsqrt(energy + EPS) * live)

    for h in range(0, RADIX, 2):
        own = []
        gain = [sum(inside[h + e][b] * gains[b] for b in range(NBANDS)) for e in range(2)]
        for b in range(NBANDS):
            pair = []
            for e in range(2):
                mask = inside[h + e][b]
                for earlier in range(b):
                    mask = mask * (1.0 - inside[h + e][earlier])
                pair.append(mask)
            own.append(jnp.concatenate(pair, axis=1).astype(bf16))
        for k in range(2):
            value = jnp.concatenate([parts[h + e][k] * gain[e] for e in range(2)], axis=1)
            value = value.astype(bf16)
            for b in range(NBANDS):
                at = (2 * b + k) * ch
                kept[at : at + ch, h * BIG : (h + 2) * BIG] = value * own[b]
    compact = jnp.dot(kept[...], joined(fold_ref), preferred_element_type=f32).astype(bf16)
    side = jnp.concatenate([compact[at : at + ch] for at in range(0, 2 * NBANDS * ch, ch)], axis=1)
    order = order_ref[...][:, :ch]
    ordered = jnp.dot(order, side, preferred_element_type=f32).astype(bf16)
    for b in range(NBANDS):
        for k in range(2):
            at = (2 * b + k) * SLOT
            sent_ref[k, :, b * SLOT : (b + 1) * SLOT] = ordered[:, at : at + SLOT]


def spectra(records, fir_taps, bands, station_live):
    ns, nw, nc, _ = records.shape
    x = jnp.transpose(records, (0, 2, 1, 3)).reshape(ns * nc, nw, RAW)
    groups = ns * nc
    padded = -(-groups // 4) * 4
    if padded != groups:
        x = jnp.pad(x, ((0, padded - groups), (0, 0), (0, 0)))
    ch = padded * nw
    hbm = pl.BlockSpec(memory_space=pltpu.HBM)
    operands = (x, fir_taps.reshape(1, TAPS), bands, station_live.reshape(1, ns))
    order = np.zeros((nw * groups, -(-ch // 128) * 128), np.float32)
    for w in range(nw):
        for i in range(groups):
            order[w * groups + i, i * nw + w] = 1.0
    operands += spectra_constants() + (order.astype(bf16),)
    return pl.pallas_call(
        spectra_kernel,
        out_shape=jax.ShapeDtypeStruct((2, nw * groups, KEPT), bf16),
        in_specs=[hbm] * len(operands),
        out_specs=pl.BlockSpec(memory_space=pltpu.VMEM),
        scratch_shapes=[pltpu.VMEM(o.shape, o.dtype) for o in operands]
        + [
            pltpu.VMEM((RADIX * ch, 2 * INNER), bf16),
            pltpu.VMEM((2 * NBANDS * ch, BINS), bf16),
            pltpu.SemaphoreType.DMA((len(operands) - 1 + PIECES,)),
        ],
        compiler_params=pltpu.CompilerParams(vmem_limit_bytes=62 * 2**20),
        cost_estimate=pl.CostEstimate(
            flops=3 * 10**9, bytes_accessed=5 * 2**20, transcendentals=0
        ),
        name="spectra",
    )(*operands)


def prepare_kernel(peers, bands_ref, sent_ref, turned_ref):
    _, nw, groups, group_rows, _ = turned_ref.shape
    repeats = group_rows // peers
    local_rows = groups * repeats
    place = lax.broadcasted_iota(jnp.int32, (1, SLOT), 1)
    residue = RADIX * (place % FOLD) + place // FOLD
    for b in range(NBANDS):
        start = bands_ref[0, b]
        f = start + ((residue - start) & (SLOT - 1))
        phase = f.astype(f32) * (math.pi / NT)
        c, sn = jnp.cos(phase), jnp.sin(phase)
        where = slice(b * SLOT, (b + 1) * SLOT)
        re, im = sent_ref[0, :, where].astype(f32), sent_ref[1, :, where].astype(f32)
        for k, value in enumerate((re * c + im * sn, im * c - re * sn)):
            for w in range(nw):
                for group in range(groups):
                    rows = []
                    for i in range(group * repeats, (group + 1) * repeats):
                        at = w * local_rows + i
                        rows.append(jnp.broadcast_to(value[at : at + 1], (peers, SLOT)))
                    turned_ref[k, w, group, :, where] = jnp.concatenate(rows, axis=0).astype(bf16)


def prepare(bands, sent, rows, nw):
    peers = 2 * rows
    fit = [n for n in range(1, rows + 1) if rows % n == 0 and n * peers % 16 == 0]
    repeats = fit[0] if fit else rows
    turned = (2, nw, rows // repeats, repeats * peers, KEPT)
    smem = pl.BlockSpec(memory_space=pltpu.SMEM)
    vmem = pl.BlockSpec(memory_space=pltpu.VMEM)
    return pl.pallas_call(
        functools.partial(prepare_kernel, peers),
        out_shape=jax.ShapeDtypeStruct(turned, bf16),
        in_specs=[smem, vmem],
        out_specs=vmem,
        compiler_params=pltpu.CompilerParams(vmem_limit_bytes=16 * 2**20),
        cost_estimate=pl.CostEstimate(flops=10**7, bytes_accessed=4 * 2**20, transcendentals=0),
        name="prepare",
    )(bands, sent)


def lag_kernel(bands_ref, base_ref, shift_ref, even_ref, odd_ref):
    place = lax.broadcasted_iota(jnp.int32, (SLOT, 1), 0)
    residue = RADIX * (place % FOLD) + place // FOLD
    for b in range(NBANDS):
        start = bands_ref[0, b]
        block = start // SLOT
        first = residue >= start % SLOT
        rows = [
            [shift_ref[k, pl.ds(block + step, 1), :] for step in range(2)] for k in range(2)
        ]
        c = jnp.where(first, rows[0][0], rows[0][1])
        s = jnp.where(first, rows[1][0], rows[1][1])
        weight = jnp.where(first & (residue + block * SLOT == 0), 0.5, 1.0)
        bc, bs = base_ref[0] * weight, base_ref[1] * weight
        even_ref[b * SLOT : (b + 1) * SLOT, :] = (bc * c - bs * s).astype(bf16)
        odd_ref[b * SLOT : (b + 1) * SLOT, :] = (bs * c + bc * s).astype(bf16)


def lag_tables(bands):
    base, shift = lag_constants()
    table = jax.ShapeDtypeStruct((KEPT, HALF), bf16)
    smem = pl.BlockSpec(memory_space=pltpu.SMEM)
    vmem = pl.BlockSpec(memory_space=pltpu.VMEM)
    return pl.pallas_call(
        lag_kernel,
        out_shape=[table, table],
        in_specs=[smem, vmem, vmem],
        out_specs=[vmem, vmem],
        compiler_params=pltpu.CompilerParams(vmem_limit_bytes=16 * 2**20),
        cost_estimate=pl.CostEstimate(flops=10**7, bytes_accessed=4 * 2**20, transcendentals=0),
        name="lag_tables",
    )(bands, base, shift)


def crossed(nw, rows, live, lanes, turned_ref, near_ref, swap_ref, cross_re, cross_im):
    _, _, groups, group_rows, _ = turned_ref.shape
    even_core = lax.rem(lax.axis_index("sta"), 2) == 0
    remote = []
    for k in range(2):
        near, swap = near_ref[k, :, lanes], swap_ref[k, :, lanes]
        by_core = [
            jnp.where(even_core, near, swap).astype(f32) * live,
            jnp.where(even_core, swap, near).astype(f32) * live,
        ]
        remote.append([])
        for w in range(nw):
            span = slice(w * rows, (w + 1) * rows)
            peers = jnp.concatenate([made[span] for made in by_core], axis=0)
            repeats = group_rows // (2 * rows)
            remote[k].append(jnp.concatenate([peers] * repeats, axis=0).astype(bf16))
    for row in range(0, group_rows, 16):
        end = min(row + 16, group_rows)
        there = [
            [remote[k][w][row:end] for w in range(nw)]
            for k in range(2)
        ]
        for group in range(groups):
            re, im = [], []
            for w in range(nw):
                lr = turned_ref[0, w, group, row:end, lanes]
                li = turned_ref[1, w, group, row:end, lanes]
                rr, ri = there[0][w], there[1][w]
                re.append(lr * rr + li * ri)
                im.append(li * rr - lr * ri)
            at = slice(group * group_rows + row, group * group_rows + end)
            cross_re[at, lanes] = (re[0] + re[1]) + (re[2] + re[3])
            cross_im[at, lanes] = (im[0] + im[1]) + (im[2] + im[3])


def mirrored(i, even, odd, value_ref):
    _, peers, _ = value_ref.shape
    backward = 127 - lax.broadcasted_iota(jnp.int32, (peers, 128), 1)
    middle = LAGS // 256
    for tile in range(HALF // 128):
        lanes = slice(tile * 128, (tile + 1) * 128)
        e, o = even[:, lanes], odd[:, lanes]
        after, before = (middle + tile) * 128, (middle - 1 - tile) * 128
        value_ref[i, :, after : after + 128] = e - o
        value_ref[i, :, before : before + 128] = jnp.take_along_axis(e + o, backward, axis=1)


def started(i, value_ref, out_ref, block, distance, sems):
    _, chips, _, _, _ = out_ref.shape
    chip = lax.rem(lax.axis_index("sta") // 2 + chips - distance, chips)
    copy = pltpu.make_async_copy(value_ref.at[i], out_ref.at[i, chip, :, block, :], sems.at[i])
    copy.start()
    return copy


def correlate_kernel(nw, units, aliased, live_ref, turned_ref, even_ref, odd_ref, *rest):
    sources, rest = rest[: 2 * len(units)], rest[2 * len(units) :]
    if aliased:
        rest = rest[1:]
    out_ref, cross_re, cross_im, values, sems = rest
    rows = out_ref.shape[0]
    total = turned_ref.shape[2] * turned_ref.shape[3]
    peers = total // rows
    bands = [slice(band * SLOT, (band + 1) * SLOT) for band in range(NBANDS)]
    copies = []

    def cross(at, band):
        crossed(
            nw,
            rows,
            live_ref[:, units[at][0] : units[at][0] + 1].astype(f32),
            bands[band],
            turned_ref,
            *sources[2 * at : 2 * at + 2],
            cross_re.at[at],
            cross_im.at[at],
        )

    def summed(at, lanes):
        even = jnp.dot(cross_re[at, :, lanes], even_ref[lanes, :], preferred_element_type=f32)
        odd = jnp.dot(cross_im[at, :, lanes], odd_ref[lanes, :], preferred_element_type=f32)
        return even, odd

    def finished(at, even, odd):
        block, distance = units[at]
        for i in range(rows):
            span = slice(i * peers, (i + 1) * peers)
            mirrored(i, even[span], odd[span], values.at[at])
            copies.append(started(i, values.at[at], out_ref, block, distance, sems.at[at]))

    if len(units) == 1:
        half = NBANDS // 2
        parts = []
        for first in (0, half):
            for band in range(first, first + half):
                cross(0, band)
            parts.append(summed(0, slice(first * SLOT, (first + half) * SLOT)))
        (even, odd), (more_even, more_odd) = parts
        finished(0, even + more_even, odd + more_odd)
    else:
        for at in range(len(units) + 1):
            if at < len(units):
                for band in range(NBANDS):
                    cross(at, band)
            if at:
                finished(at - 1, *summed(at - 1, slice(0, KEPT)))
    for copy in copies:
        copy.wait()


def correlate(block_live, turned, tables, rows, chips, units, sources, more=()):
    _, nw, groups, group_rows, _ = turned.shape
    total = groups * group_rows
    peers = 2 * rows
    n = len(units)
    vmem = pl.BlockSpec(memory_space=pltpu.VMEM)
    output = pl.BlockSpec(memory_space=pl.ANY)
    operands = [block_live, turned, *tables, *sources]
    cross = pltpu.VMEM((n, total, KEPT), bf16)
    return pl.pallas_call(
        functools.partial(correlate_kernel, nw, units, bool(more)),
        out_shape=jax.ShapeDtypeStruct((rows, chips, peers, OFFS, LAGS), f32),
        in_specs=[vmem] * len(operands) + [output] * len(more),
        out_specs=output,
        scratch_shapes=[
            cross,
            cross,
            pltpu.VMEM((n, rows, peers, LAGS), f32),
            pltpu.SemaphoreType.DMA((n, rows)),
        ],
        input_output_aliases={len(operands): 0} if more else {},
        compiler_params=pltpu.CompilerParams(vmem_limit_bytes=(24 if more else 32) * 2**20),
        cost_estimate=pl.CostEstimate(
            flops=4 * n * total * KEPT * HALF,
            bytes_accessed=8 * 2**20,
            transcendentals=0,
        ),
        name="block_rows",
    )(*operands, *more)


def next_group(block):
    axes = ("section", "grp")
    n = lax.axis_size(axes)
    return lax.ppermute(block, axes, [((i - 1) % n, i) for i in range(n)])


def swapped_core(block):
    n = lax.axis_size("sta")
    return lax.ppermute(block, "sta", [(i, i ^ 1) for i in range(n)])


def from_chip(block, distance):
    n = lax.axis_size("sta")
    return lax.ppermute(block, "sta", [(i, (i + 2 * distance) % n) for i in range(n)])


def tied(*values):
    return lax.optimization_barrier(values)


def body(records, fir_taps, band_bins, station_live, block_live):
    chips = lax.axis_size("sta") // 2
    ns, nw, nc, _ = records.shape
    rows = ns * nc
    bands = jnp.transpose(band_bins)
    sent = spectra(records, fir_taps, bands, station_live)
    turned = prepare(bands, sent, rows, nw)
    tables = lag_tables(bands)
    first, turned, *tables = tied(next_group(sent), turned, *tables)
    second = next_group(first)
    far = [from_chip(first, d) for d in range(1, chips)]
    near_swap = swapped_core(first)
    far, second = tied(far, second)
    held = [first, near_swap]
    for block in far:
        held += [block, swapped_core(block)]
    far_second = [from_chip(second, d) for d in range(1, chips)]
    near_swap = swapped_core(second)
    live = block_live.reshape(1, OFFS)

    def written(units, held, *more):
        return correlate(live, turned, tables, rows, chips, units, held, more)

    units = [(0, d) for d in range(chips)] + [(1, 0)]
    result = written(units, held + [second, near_swap])
    far_second, result = tied(far_second, result)
    for d in range(1, chips):
        far = far_second[d - 1]
        result = written([(1, d)], [far, swapped_core(far)], result)
    return result.reshape(-1, OFFS, LAGS)


def solution(mesh):
    in_specs = (
        P(("section", "grp", "sta"), None, None, None),
        P(),
        P(),
        P(("section", "grp", "sta")),
        P(("section", "grp")),
    )
    out_specs = P("sta", ("section", "grp"), None)
    return jax.shard_map(body, mesh=mesh, in_specs=in_specs, out_specs=out_specs, check_vma=False)
```

```python
import functools
import math

import jax
import jax.numpy as jnp
import numpy as np
from jax import lax
from jax.experimental import pallas as pl
from jax.experimental.pallas import tpu as pltpu
from jax.sharding import PartitionSpec as P

BINS = 2048
NT = 4096
DEC = 4
RAW = 16384
TAPS = 64
NBANDS = 4
SLOT = 256
OFFS = 2
LAGS = 1024
HALF = LAGS // 2
RADIX = 16
INNER = NT // RADIX
BIG = BINS // RADIX
FOLD = 256 // RADIX
FRAME = 128
SPAN = DEC * FRAME
LEAD = 256
WINDOW = SPAN + LEAD
PIECES = 4
BLOCKS_IN = NT // FRAME
KEPT = NBANDS * SLOT
EPS = 1e-06

f32 = jnp.float32
bf16 = jnp.bfloat16


def by_tile(table):
    padded = np.pad(table, ((0, 0), (0, -table.shape[1] % 128)))
    return np.ascontiguousarray(
        padded.reshape(table.shape[0], -1, 128).transpose(1, 0, 2)
    )


def joined(ref):
    return jnp.concatenate([ref[i] for i in range(ref.shape[0])], axis=1)


def compact_order():
    place = np.arange(SLOT)
    return RADIX * (place % FOLD) + place // FOLD


def spectra_constants():
    inner = np.arange(INNER)
    g = np.arange(BIG)
    angle = 2.0 * np.pi * ((inner[:, None] * g[None, :]) % INNER) / INNER
    cos, sin = np.cos(angle), np.sin(angle)
    table = np.concatenate(
        [np.concatenate([cos, -sin], axis=1), np.concatenate([sin, cos], axis=1)], axis=0
    )
    h = np.arange(RADIX)
    turn = 2.0 * np.pi * (h[:, None] * inner[None, :]) / NT
    twiddle = np.stack([np.cos(turn), -np.sin(turn)]).astype(np.float32)
    place = np.zeros((TAPS, WINDOW), np.float32)
    place[np.arange(TAPS), LEAD - np.arange(TAPS)] = 1.0
    fold = np.zeros((RADIX, BIG, SLOT), np.float32)
    for step in range(RADIX):
        fold[step, np.arange(BIG), FOLD * step + np.arange(BIG) % FOLD] = 1.0
    fold = by_tile(fold.reshape(BINS, SLOT).astype(bf16))
    return by_tile(table.astype(np.float32).astype(bf16)), twiddle, by_tile(place.astype(bf16)), fold


def lag_constants():
    q = compact_order()[:, None].astype(np.float64)
    n = np.arange(HALF)[None, :] + 0.5
    angle = 2.0 * np.pi * ((q * 2 * n) % (2 * NT)) / (2 * NT)
    base = np.stack([np.cos(angle), np.sin(angle)]) / math.sqrt(BINS)
    block = np.arange(16)[:, None].astype(np.float64)
    turn = 2.0 * np.pi * ((block * SLOT * 2 * n) % (2 * NT)) / (2 * NT)
    shift = np.stack([np.cos(turn), np.sin(turn)])
    return base.astype(np.float32), shift.astype(np.float32)


def real_dft8(d):
    r = math.sqrt(0.5)
    s = [d[b] + d[b + 4] for b in range(4)]
    t = [d[b] - d[b + 4] for b in range(4)]
    s02, s13 = s[0] + s[2], s[1] + s[3]
    t13m, t13p = r * (t[1] - t[3]), r * (t[1] + t[3])
    return [
        (s02 + s13, None),
        (t[0] + t13m, -(t[2] + t13p)),
        (s[0] - s[2], s[3] - s[1]),
        (t[0] - t13m, t[2] - t13p),
        (s02 - s13, None),
    ]


def real_dft16(d):
    even, odd = real_dft8(d[0::2]), real_dft8(d[1::2])
    y = [None] * 16
    y[0] = (even[0][0] + odd[0][0], None)
    y[8] = (even[0][0] - odd[0][0], None)
    y[4] = (even[4][0], -odd[4][0])
    for h in range(1, 4):
        c, s = math.cos(math.pi * h / 8), -math.sin(math.pi * h / 8)
        re, im = odd[h]
        tr, ti = re * c - im * s, re * s + im * c
        y[h] = (even[h][0] + tr, even[h][1] + ti)
        y[8 - h] = (even[h][0] - tr, ti - even[h][1])
    for h in range(9, 16):
        y[h] = (y[16 - h][0], -y[16 - h][1])
    return y


def spectra_kernel(
    x_hbm,
    taps_hbm,
    bands_hbm,
    live_hbm,
    table_hbm,
    twiddle_hbm,
    place_hbm,
    fold_hbm,
    order_hbm,
    sent_ref,
    x_ref,
    taps_ref,
    bands_ref,
    live_ref,
    table_ref,
    twiddle_ref,
    place_ref,
    fold_ref,
    order_ref,
    turned,
    kept,
    sems,
):
    ch = x_ref.shape[0] * x_ref.shape[1]
    piece = RAW // PIECES
    pairs = [(taps_hbm, taps_ref), (place_hbm, place_ref)]
    for i in range(PIECES):
        lanes = slice(i * piece, (i + 1) * piece)
        pairs.append((x_hbm.at[:, :, lanes], x_ref.at[:, :, lanes]))
    pairs += [
        (twiddle_hbm, twiddle_ref),
        (table_hbm, table_ref),
        (bands_hbm, bands_ref),
        (live_hbm, live_ref),
        (fold_hbm, fold_ref),
        (order_hbm, order_ref),
    ]
    copies = [pltpu.make_async_copy(a, b, sems.at[i]) for i, (a, b) in enumerate(pairs)]
    for copy in copies:
        copy.start()
    copies[0].wait()
    taps = taps_ref[...]
    copies[1].wait()
    taps_high = taps.astype(bf16)
    taps_low = (taps - taps_high.astype(f32)).astype(bf16)

    def toeplitz(part):
        row = jnp.dot(part, joined(place_ref), preferred_element_type=f32)
        return pltpu.roll(
            jnp.broadcast_to(row, (FRAME, WINDOW)), 0, 1, stride=DEC, stride_axis=0
        ).astype(bf16)

    weights = jnp.concatenate([toeplitz(taps_high), toeplitz(taps_low)], axis=0)
    decimated = []
    tail = jnp.zeros((ch, LEAD), bf16)
    for i in range(PIECES):
        copies[2 + i].wait()
        x = x_ref[:, :, i * piece : (i + 1) * piece].reshape(ch, piece)
        x = jnp.concatenate([tail, x], axis=1)
        tail = x[:, piece:]
        windows = [x[:, at : at + WINDOW] for at in range(0, piece, SPAN)]
        both = lax.dot_general(
            jnp.concatenate(windows, axis=0),
            weights,
            (((1,), (1,)), ((), ())),
            preferred_element_type=f32,
        )
        decimated.append((both[:, :FRAME] + both[:, FRAME:]).astype(bf16).astype(f32))
    each = BLOCKS_IN // PIECES
    copies[2 + PIECES].wait()
    for at in range(0, ch, 16):
        d = []
        for b in range(RADIX):
            pair = []
            for frame in (2 * b, 2 * b + 1):
                row = frame % each * ch + at
                pair.append(decimated[frame // each][row : row + 16])
            d.append(jnp.concatenate(pair, axis=1))
        y = real_dft16(d)
        for h in range(RADIX):
            c = twiddle_ref[0, h : h + 1, :]
            sn = twiddle_ref[1, h : h + 1, :]
            yr, yi = y[h]
            if yi is None:
                ur, ui = yr * c, yr * sn
            else:
                ur, ui = yr * c - yi * sn, yr * sn + yi * c
            for k, u in enumerate((ur, ui)):
                where = slice(k * INNER, (k + 1) * INNER)
                turned[h * ch + at : h * ch + at + 16, where] = u.astype(bf16)

    for copy in copies[3 + PIECES :]:
        copy.wait()
    spectrum = jnp.dot(turned[...], joined(table_ref), preferred_element_type=f32)

    row = lax.broadcasted_iota(jnp.int32, (ch, 1), 0)
    station = row // 12
    live = jnp.zeros((ch, 1), f32)
    station_live = live_ref[...].astype(f32)
    for s_at in range(live_ref.shape[1]):
        live = jnp.where(station == s_at, station_live[:, s_at : s_at + 1], live)
    bands = bands_ref[...]
    edges = [[bands[k : k + 1, b : b + 1] for b in range(NBANDS)] for k in range(2)]

    g = lax.broadcasted_iota(jnp.int32, (1, BIG), 1)
    inside = []
    for h in range(RADIX):
        f = RADIX * g + h
        inside.append(
            [
                ((f >= edges[0][b]) & (f < edges[1][b])).astype(f32)
                for b in range(NBANDS)
            ]
        )
    parts = []
    sums = [jnp.zeros((ch, BIG), f32) for _ in range(NBANDS)]
    for h in range(RADIX):
        re = spectrum[h * ch : (h + 1) * ch, :BIG]
        im = spectrum[h * ch : (h + 1) * ch, BIG:]
        parts.append((re, im))
        power = re * re + im * im
        for b in range(NBANDS):
            sums[b] = sums[b] + power * inside[h][b]
    gains = []
    for b in range(NBANDS):
        width = (edges[1][b] - edges[0][b]).astype(f32)
        energy = jnp.sum(sums[b], axis=1, keepdims=True) / width
        gains.append(lax.rsqrt(energy + EPS) * live)

    for h in range(0, RADIX, 2):
        own = []
        gain = [sum(inside[h + e][b] * gains[b] for b in range(NBANDS)) for e in range(2)]
        for b in range(NBANDS):
            pair = []
            for e in range(2):
                mask = inside[h + e][b]
                for earlier in range(b):
                    mask = mask * (1.0 - inside[h + e][earlier])
                pair.append(mask)
            own.append(jnp.concatenate(pair, axis=1).astype(bf16))
        for k in range(2):
            value = jnp.concatenate([parts[h + e][k] * gain[e] for e in range(2)], axis=1)
            value = value.astype(bf16)
            for b in range(NBANDS):
                at = (2 * b + k) * ch
                kept[at : at + ch, h * BIG : (h + 2) * BIG] = value * own[b]
    compact = jnp.dot(kept[...], joined(fold_ref), preferred_element_type=f32).astype(bf16)
    side = jnp.concatenate([compact[at : at + ch] for at in range(0, 2 * NBANDS * ch, ch)], axis=1)
    order = order_ref[...][:, :ch]
    ordered = jnp.dot(order, side, preferred_element_type=f32).astype(bf16)
    for b in range(NBANDS):
        for k in range(2):
            at = (2 * b + k) * SLOT
            sent_ref[k, :, b * SLOT : (b + 1) * SLOT] = ordered[:, at : at + SLOT]


def spectra(records, fir_taps, bands, station_live):
    ns, nw, nc, _ = records.shape
    x = jnp.transpose(records, (0, 2, 1, 3)).reshape(ns * nc, nw, RAW)
    groups = ns * nc
    padded = -(-groups // 4) * 4
    if padded != groups:
        x = jnp.pad(x, ((0, padded - groups), (0, 0), (0, 0)))
    ch = padded * nw
    hbm = pl.BlockSpec(memory_space=pltpu.HBM)
    operands = (x, fir_taps.reshape(1, TAPS), bands, station_live.reshape(1, ns))
    order = np.zeros((nw * groups, -(-ch // 128) * 128), np.float32)
    for w in range(nw):
        for i in range(groups):
            order[w * groups + i, i * nw + w] = 1.0
    operands += spectra_constants() + (order.astype(bf16),)
    return pl.pallas_call(
        spectra_kernel,
        out_shape=jax.ShapeDtypeStruct((2, nw * groups, KEPT), bf16),
        in_specs=[hbm] * len(operands),
        out_specs=pl.BlockSpec(memory_space=pltpu.VMEM),
        scratch_shapes=[pltpu.VMEM(o.shape, o.dtype) for o in operands]
        + [
            pltpu.VMEM((RADIX * ch, 2 * INNER), bf16),
            pltpu.VMEM((2 * NBANDS * ch, BINS), bf16),
            pltpu.SemaphoreType.DMA((len(operands) - 1 + PIECES,)),
        ],
        compiler_params=pltpu.CompilerParams(vmem_limit_bytes=62 * 2**20),
        cost_estimate=pl.CostEstimate(
            flops=3 * 10**9, bytes_accessed=5 * 2**20, transcendentals=0
        ),
        name="spectra",
    )(*operands)


def prepare_kernel(peers, bands_ref, sent_ref, turned_ref):
    _, nw, groups, group_rows, _ = turned_ref.shape
    repeats = group_rows // peers
    local_rows = groups * repeats
    place = lax.broadcasted_iota(jnp.int32, (1, SLOT), 1)
    residue = RADIX * (place % FOLD) + place // FOLD
    for b in range(NBANDS):
        start = bands_ref[0, b]
        f = start + ((residue - start) & (SLOT - 1))
        phase = f.astype(f32) * (math.pi / NT)
        c, sn = jnp.cos(phase), jnp.sin(phase)
        where = slice(b * SLOT, (b + 1) * SLOT)
        re, im = sent_ref[0, :, where].astype(f32), sent_ref[1, :, where].astype(f32)
        for k, value in enumerate((re * c + im * sn, im * c - re * sn)):
            for w in range(nw):
                for group in range(groups):
                    rows = []
                    for i in range(group * repeats, (group + 1) * repeats):
                        at = w * local_rows + i
                        rows.append(jnp.broadcast_to(value[at : at + 1], (peers, SLOT)))
                    turned_ref[k, w, group, :, where] = jnp.concatenate(rows, axis=0).astype(bf16)


def prepare(bands, sent, rows, nw):
    peers = 2 * rows
    fit = [n for n in range(1, rows + 1) if rows % n == 0 and n * peers % 16 == 0]
    repeats = fit[0] if fit else rows
    turned = (2, nw, rows // repeats, repeats * peers, KEPT)
    smem = pl.BlockSpec(memory_space=pltpu.SMEM)
    vmem = pl.BlockSpec(memory_space=pltpu.VMEM)
    return pl.pallas_call(
        functools.partial(prepare_kernel, peers),
        out_shape=jax.ShapeDtypeStruct(turned, bf16),
        in_specs=[smem, vmem],
        out_specs=vmem,
        compiler_params=pltpu.CompilerParams(vmem_limit_bytes=16 * 2**20),
        cost_estimate=pl.CostEstimate(flops=10**7, bytes_accessed=4 * 2**20, transcendentals=0),
        name="prepare",
    )(bands, sent)


def lag_kernel(bands_ref, base_ref, shift_ref, even_ref, odd_ref):
    place = lax.broadcasted_iota(jnp.int32, (SLOT, 1), 0)
    residue = RADIX * (place % FOLD) + place // FOLD
    for b in range(NBANDS):
        start = bands_ref[0, b]
        block = start // SLOT
        first = residue >= start % SLOT
        rows = [
            [shift_ref[k, pl.ds(block + step, 1), :] for step in range(2)] for k in range(2)
        ]
        c = jnp.where(first, rows[0][0], rows[0][1])
        s = jnp.where(first, rows[1][0], rows[1][1])
        weight = jnp.where(first & (residue + block * SLOT == 0), 0.5, 1.0)
        bc, bs = base_ref[0] * weight, base_ref[1] * weight
        even_ref[b * SLOT : (b + 1) * SLOT, :] = (bc * c - bs * s).astype(bf16)
        odd_ref[b * SLOT : (b + 1) * SLOT, :] = (bs * c + bc * s).astype(bf16)


def lag_tables(bands):
    base, shift = lag_constants()
    table = jax.ShapeDtypeStruct((KEPT, HALF), bf16)
    smem = pl.BlockSpec(memory_space=pltpu.SMEM)
    vmem = pl.BlockSpec(memory_space=pltpu.VMEM)
    return pl.pallas_call(
        lag_kernel,
        out_shape=[table, table],
        in_specs=[smem, vmem, vmem],
        out_specs=[vmem, vmem],
        compiler_params=pltpu.CompilerParams(vmem_limit_bytes=16 * 2**20),
        cost_estimate=pl.CostEstimate(flops=10**7, bytes_accessed=4 * 2**20, transcendentals=0),
        name="lag_tables",
    )(bands, base, shift)


def crossed(nw, rows, live, lanes, turned_ref, near_ref, swap_ref, cross_re, cross_im):
    _, _, groups, group_rows, _ = turned_ref.shape
    even_core = lax.rem(lax.axis_index("sta"), 2) == 0
    remote = []
    for k in range(2):
        near, swap = near_ref[k, :, lanes], swap_ref[k, :, lanes]
        by_core = [
            jnp.where(even_core, near, swap).astype(f32) * live,
            jnp.where(even_core, swap, near).astype(f32) * live,
        ]
        remote.append([])
        for w in range(nw):
            span = slice(w * rows, (w + 1) * rows)
            peers = jnp.concatenate([made[span] for made in by_core], axis=0)
            repeats = group_rows // (2 * rows)
            remote[k].append(jnp.concatenate([peers] * repeats, axis=0).astype(bf16))
    for row in range(0, group_rows, 16):
        end = min(row + 16, group_rows)
        there = [
            [remote[k][w][row:end] for w in range(nw)]
            for k in range(2)
        ]
        for group in range(groups):
            re, im = [], []
            for w in range(nw):
                lr = turned_ref[0, w, group, row:end, lanes]
                li = turned_ref[1, w, group, row:end, lanes]
                rr, ri = there[0][w], there[1][w]
                re.append(lr * rr + li * ri)
                im.append(li * rr - lr * ri)
            at = slice(group * group_rows + row, group * group_rows + end)
            cross_re[at, lanes] = (re[0] + re[1]) + (re[2] + re[3])
            cross_im[at, lanes] = (im[0] + im[1]) + (im[2] + im[3])


def mirrored(i, columns, even, odd, value_ref):
    peers, width = even.shape
    backward = 127 - lax.broadcasted_iota(jnp.int32, (peers, 128), 1)
    for tile in range(0, width, 128):
        e, o = even[:, tile : tile + 128], odd[:, tile : tile + 128]
        after = pl.multiple_of(HALF + columns + tile, 128)
        before = pl.multiple_of(HALF - columns - tile - 128, 128)
        value_ref[i, :, pl.ds(after, 128)] = e - o
        value_ref[i, :, pl.ds(before, 128)] = jnp.take_along_axis(e + o, backward, axis=1)


def started(i, value_ref, out_ref, block, distance, sems):
    _, chips, _, _, _ = out_ref.shape
    chip = lax.rem(lax.axis_index("sta") // 2 + chips - distance, chips)
    copy = pltpu.make_async_copy(value_ref.at[i], out_ref.at[i, chip, :, block, :], sems.at[i])
    copy.start()
    return copy


def correlate_kernel(nw, units, aliased, live_ref, turned_ref, even_ref, odd_ref, *rest):
    sources, rest = rest[: 2 * len(units)], rest[2 * len(units) :]
    if aliased:
        rest = rest[1:]
    out_ref, cross_re, cross_im, values, sems = rest
    rows = out_ref.shape[0]
    total = turned_ref.shape[2] * turned_ref.shape[3]
    peers = total // rows
    copies = []
    width = HALF // 2
    for at, (block, distance) in enumerate(units):
        live = live_ref[:, block : block + 1].astype(f32)

        @pl.loop(0, NBANDS)
        def cross(band):
            crossed(
                nw,
                rows,
                live,
                pl.ds(pl.multiple_of(band * SLOT, SLOT), SLOT),
                turned_ref,
                *sources[2 * at : 2 * at + 2],
                cross_re.at[at],
                cross_im.at[at],
            )

        @pl.loop(0, HALF // width)
        def lags(step):
            columns = pl.multiple_of(step * width, width)
            some = pl.ds(columns, width)
            even = jnp.dot(cross_re[at], even_ref[:, some], preferred_element_type=f32)
            odd = jnp.dot(cross_im[at], odd_ref[:, some], preferred_element_type=f32)
            for i in range(rows):
                span = slice(i * peers, (i + 1) * peers)
                mirrored(i, columns, even[span], odd[span], values.at[at])

        for i in range(rows):
            copies.append(started(i, values.at[at], out_ref, block, distance, sems.at[at]))
    for copy in copies:
        copy.wait()


def correlate(block_live, turned, tables, rows, chips, units, sources, more=()):
    _, nw, groups, group_rows, _ = turned.shape
    total = groups * group_rows
    peers = 2 * rows
    n = len(units)
    vmem = pl.BlockSpec(memory_space=pltpu.VMEM)
    output = pl.BlockSpec(memory_space=pl.ANY)
    operands = [block_live, turned, *tables, *sources]
    cross = pltpu.VMEM((n, total, KEPT), bf16)
    return pl.pallas_call(
        functools.partial(correlate_kernel, nw, units, bool(more)),
        out_shape=jax.ShapeDtypeStruct((rows, chips, peers, OFFS, LAGS), f32),
        in_specs=[vmem] * len(operands) + [output] * len(more),
        out_specs=output,
        scratch_shapes=[
            cross,
            cross,
            pltpu.VMEM((n, rows, peers, LAGS), f32),
            pltpu.SemaphoreType.DMA((n, rows)),
        ],
        input_output_aliases={len(operands): 0} if more else {},
        compiler_params=pltpu.CompilerParams(vmem_limit_bytes=(24 if more else 32) * 2**20),
        cost_estimate=pl.CostEstimate(
            flops=4 * n * total * KEPT * HALF,
            bytes_accessed=8 * 2**20,
            transcendentals=0,
        ),
        name="block_rows",
    )(*operands, *more)


def next_group(block):
    axes = ("section", "grp")
    n = lax.axis_size(axes)
    return lax.ppermute(block, axes, [((i - 1) % n, i) for i in range(n)])


def swapped_core(block):
    n = lax.axis_size("sta")
    return lax.ppermute(block, "sta", [(i, i ^ 1) for i in range(n)])


def from_chip(block, distance):
    n = lax.axis_size("sta")
    return lax.ppermute(block, "sta", [(i, (i + 2 * distance) % n) for i in range(n)])


def tied(*values):
    return lax.optimization_barrier(values)


def body(records, fir_taps, band_bins, station_live, block_live):
    chips = lax.axis_size("sta") // 2
    ns, nw, nc, _ = records.shape
    rows = ns * nc
    bands = jnp.transpose(band_bins)
    sent = spectra(records, fir_taps, bands, station_live)
    turned = prepare(bands, sent, rows, nw)
    tables = lag_tables(bands)
    first, turned, *tables = tied(next_group(sent), turned, *tables)
    second = next_group(first)
    far = [from_chip(first, d) for d in range(1, chips)]
    near_swap = swapped_core(first)
    far, second = tied(far, second)
    held = [first, near_swap]
    for block in far:
        held += [block, swapped_core(block)]
    far_second = [from_chip(second, d) for d in range(1, chips)]
    near_swap = swapped_core(second)
    live = block_live.reshape(1, OFFS)

    def written(units, held, *more):
        return correlate(live, turned, tables, rows, chips, units, held, more)

    units = [(0, d) for d in range(chips)] + [(1, 0)]
    result = written(units, held + [second, near_swap])
    far_second, result = tied(far_second, result)
    for d in range(1, chips):
        far = far_second[d - 1]
        result = written([(1, d)], [far, swapped_core(far)], result)
    return result.reshape(-1, OFFS, LAGS)


def solution(mesh):
    in_specs = (
        P(("section", "grp", "sta"), None, None, None),
        P(),
        P(),
        P(("section", "grp", "sta")),
        P(("section", "grp")),
    )
    out_specs = P("sta", ("section", "grp"), None)
    return jax.shard_map(body, mesh=mesh, in_specs=in_specs, out_specs=out_specs, check_vma=False)
```

```python
import functools
import math

import jax
import jax.numpy as jnp
import numpy as np
from jax import lax
from jax.experimental import pallas as pl
from jax.experimental.pallas import tpu as pltpu
from jax.sharding import PartitionSpec as P

BINS = 2048
NT = 4096
DEC = 4
RAW = 16384
TAPS = 64
NBANDS = 4
SLOT = 256
OFFS = 2
LAGS = 1024
HALF = LAGS // 2
RADIX = 16
INNER = NT // RADIX
BIG = BINS // RADIX
FOLD = 256 // RADIX
FRAME = 128
SPAN = DEC * FRAME
LEAD = 256
WINDOW = SPAN + LEAD
PIECES = 4
BLOCKS_IN = NT // FRAME
KEPT = NBANDS * SLOT
EPS = 1e-06

f32 = jnp.float32
bf16 = jnp.bfloat16


def by_tile(table):
    padded = np.pad(table, ((0, 0), (0, -table.shape[1] % 128)))
    return np.ascontiguousarray(
        padded.reshape(table.shape[0], -1, 128).transpose(1, 0, 2)
    )


def joined(ref):
    return jnp.concatenate([ref[i] for i in range(ref.shape[0])], axis=1)


def compact_order():
    place = np.arange(SLOT)
    return RADIX * (place % FOLD) + place // FOLD


def spectra_constants():
    inner = np.arange(INNER)
    g = np.arange(BIG)
    angle = 2.0 * np.pi * ((inner[:, None] * g[None, :]) % INNER) / INNER
    cos, sin = np.cos(angle), np.sin(angle)
    table = np.concatenate(
        [np.concatenate([cos, -sin], axis=1), np.concatenate([sin, cos], axis=1)], axis=0
    )
    h = np.arange(RADIX)
    turn = 2.0 * np.pi * (h[:, None] * inner[None, :]) / NT
    twiddle = np.stack([np.cos(turn), -np.sin(turn)]).astype(np.float32)
    place = np.zeros((TAPS, WINDOW), np.float32)
    place[np.arange(TAPS), LEAD - np.arange(TAPS)] = 1.0
    fold = np.zeros((RADIX, BIG, SLOT), np.float32)
    for step in range(RADIX):
        fold[step, np.arange(BIG), FOLD * step + np.arange(BIG) % FOLD] = 1.0
    fold = by_tile(fold.reshape(BINS, SLOT).astype(bf16))
    return by_tile(table.astype(np.float32).astype(bf16)), twiddle, by_tile(place.astype(bf16)), fold


def lag_constants():
    q = compact_order()[:, None].astype(np.float64)
    n = np.arange(HALF)[None, :] + 0.5
    angle = 2.0 * np.pi * ((q * 2 * n) % (2 * NT)) / (2 * NT)
    base = np.stack([np.cos(angle), np.sin(angle)]) / math.sqrt(BINS)
    block = np.arange(16)[:, None].astype(np.float64)
    turn = 2.0 * np.pi * ((block * SLOT * 2 * n) % (2 * NT)) / (2 * NT)
    shift = np.stack([np.cos(turn), np.sin(turn)])
    return base.astype(np.float32), shift.astype(np.float32)


def real_dft8(d):
    r = math.sqrt(0.5)
    s = [d[b] + d[b + 4] for b in range(4)]
    t = [d[b] - d[b + 4] for b in range(4)]
    s02, s13 = s[0] + s[2], s[1] + s[3]
    t13m, t13p = r * (t[1] - t[3]), r * (t[1] + t[3])
    return [
        (s02 + s13, None),
        (t[0] + t13m, -(t[2] + t13p)),
        (s[0] - s[2], s[3] - s[1]),
        (t[0] - t13m, t[2] - t13p),
        (s02 - s13, None),
    ]


def real_dft16(d):
    even, odd = real_dft8(d[0::2]), real_dft8(d[1::2])
    y = [None] * 16
    y[0] = (even[0][0] + odd[0][0], None)
    y[8] = (even[0][0] - odd[0][0], None)
    y[4] = (even[4][0], -odd[4][0])
    for h in range(1, 4):
        c, s = math.cos(math.pi * h / 8), -math.sin(math.pi * h / 8)
        re, im = odd[h]
        tr, ti = re * c - im * s, re * s + im * c
        y[h] = (even[h][0] + tr, even[h][1] + ti)
        y[8 - h] = (even[h][0] - tr, ti - even[h][1])
    for h in range(9, 16):
        y[h] = (y[16 - h][0], -y[16 - h][1])
    return y


def spectra_kernel(
    x_hbm,
    taps_hbm,
    bands_hbm,
    live_hbm,
    table_hbm,
    twiddle_hbm,
    place_hbm,
    fold_hbm,
    order_hbm,
    sent_ref,
    x_ref,
    taps_ref,
    bands_ref,
    live_ref,
    table_ref,
    twiddle_ref,
    place_ref,
    fold_ref,
    order_ref,
    turned,
    kept,
    sems,
):
    ch = x_ref.shape[0] * x_ref.shape[1]
    piece = RAW // PIECES
    pairs = [(taps_hbm, taps_ref), (place_hbm, place_ref)]
    for i in range(PIECES):
        lanes = slice(i * piece, (i + 1) * piece)
        pairs.append((x_hbm.at[:, :, lanes], x_ref.at[:, :, lanes]))
    pairs += [
        (twiddle_hbm, twiddle_ref),
        (table_hbm, table_ref),
        (bands_hbm, bands_ref),
        (live_hbm, live_ref),
        (fold_hbm, fold_ref),
        (order_hbm, order_ref),
    ]
    copies = [pltpu.make_async_copy(a, b, sems.at[i]) for i, (a, b) in enumerate(pairs)]
    for copy in copies:
        copy.start()
    copies[0].wait()
    taps = taps_ref[...]
    copies[1].wait()
    taps_high = taps.astype(bf16)
    taps_low = (taps - taps_high.astype(f32)).astype(bf16)

    def toeplitz(part):
        row = jnp.dot(part, joined(place_ref), preferred_element_type=f32)
        return pltpu.roll(
            jnp.broadcast_to(row, (FRAME, WINDOW)), 0, 1, stride=DEC, stride_axis=0
        ).astype(bf16)

    weights = jnp.concatenate([toeplitz(taps_high), toeplitz(taps_low)], axis=0)
    decimated = []
    tail = jnp.zeros((ch, LEAD), bf16)
    for i in range(PIECES):
        copies[2 + i].wait()
        x = x_ref[:, :, i * piece : (i + 1) * piece].reshape(ch, piece)
        x = jnp.concatenate([tail, x], axis=1)
        tail = x[:, piece:]
        windows = [x[:, at : at + WINDOW] for at in range(0, piece, SPAN)]
        both = lax.dot_general(
            jnp.concatenate(windows, axis=0),
            weights,
            (((1,), (1,)), ((), ())),
            preferred_element_type=f32,
        )
        decimated.append((both[:, :FRAME] + both[:, FRAME:]).astype(bf16).astype(f32))
    each = BLOCKS_IN // PIECES
    copies[2 + PIECES].wait()
    for at in range(0, ch, 16):
        d = []
        for b in range(RADIX):
            pair = []
            for frame in (2 * b, 2 * b + 1):
                row = frame % each * ch + at
                pair.append(decimated[frame // each][row : row + 16])
            d.append(jnp.concatenate(pair, axis=1))
        y = real_dft16(d)
        for h in range(RADIX):
            c = twiddle_ref[0, h : h + 1, :]
            sn = twiddle_ref[1, h : h + 1, :]
            yr, yi = y[h]
            if yi is None:
                ur, ui = yr * c, yr * sn
            else:
                ur, ui = yr * c - yi * sn, yr * sn + yi * c
            for k, u in enumerate((ur, ui)):
                where = slice(k * INNER, (k + 1) * INNER)
                turned[h * ch + at : h * ch + at + 16, where] = u.astype(bf16)

    for copy in copies[3 + PIECES :]:
        copy.wait()
    spectrum = jnp.dot(turned[...], joined(table_ref), preferred_element_type=f32)

    row = lax.broadcasted_iota(jnp.int32, (ch, 1), 0)
    station = row // 12
    live = jnp.zeros((ch, 1), f32)
    station_live = live_ref[...].astype(f32)
    for s_at in range(live_ref.shape[1]):
        live = jnp.where(station == s_at, station_live[:, s_at : s_at + 1], live)
    bands = bands_ref[...]
    edges = [[bands[k : k + 1, b : b + 1] for b in range(NBANDS)] for k in range(2)]

    g = lax.broadcasted_iota(jnp.int32, (1, BIG), 1)
    inside = []
    for h in range(RADIX):
        f = RADIX * g + h
        inside.append(
            [
                ((f >= edges[0][b]) & (f < edges[1][b])).astype(f32)
                for b in range(NBANDS)
            ]
        )
    parts = []
    sums = [jnp.zeros((ch, BIG), f32) for _ in range(NBANDS)]
    for h in range(RADIX):
        re = spectrum[h * ch : (h + 1) * ch, :BIG]
        im = spectrum[h * ch : (h + 1) * ch, BIG:]
        parts.append((re, im))
        power = re * re + im * im
        for b in range(NBANDS):
            sums[b] = sums[b] + power * inside[h][b]
    gains = []
    for b in range(NBANDS):
        width = (edges[1][b] - edges[0][b]).astype(f32)
        energy = jnp.sum(sums[b], axis=1, keepdims=True) / width
        gains.append(lax.rsqrt(energy + EPS) * live)

    for h in range(0, RADIX, 2):
        own = []
        gain = [sum(inside[h + e][b] * gains[b] for b in range(NBANDS)) for e in range(2)]
        for b in range(NBANDS):
            pair = []
            for e in range(2):
                mask = inside[h + e][b]
                for earlier in range(b):
                    mask = mask * (1.0 - inside[h + e][earlier])
                pair.append(mask)
            own.append(jnp.concatenate(pair, axis=1).astype(bf16))
        for k in range(2):
            value = jnp.concatenate([parts[h + e][k] * gain[e] for e in range(2)], axis=1)
            value = value.astype(bf16)
            for b in range(NBANDS):
                at = (2 * b + k) * ch
                kept[at : at + ch, h * BIG : (h + 2) * BIG] = value * own[b]
    compact = jnp.dot(kept[...], joined(fold_ref), preferred_element_type=f32).astype(bf16)
    side = jnp.concatenate([compact[at : at + ch] for at in range(0, 2 * NBANDS * ch, ch)], axis=1)
    order = order_ref[...][:, :ch]
    ordered = jnp.dot(order, side, preferred_element_type=f32).astype(bf16)
    for b in range(NBANDS):
        for k in range(2):
            at = (2 * b + k) * SLOT
            sent_ref[k, :, b * SLOT : (b + 1) * SLOT] = ordered[:, at : at + SLOT]


def spectra(records, fir_taps, bands, station_live):
    ns, nw, nc, _ = records.shape
    x = jnp.transpose(records, (0, 2, 1, 3)).reshape(ns * nc, nw, RAW)
    groups = ns * nc
    padded = -(-groups // 4) * 4
    if padded != groups:
        x = jnp.pad(x, ((0, padded - groups), (0, 0), (0, 0)))
    ch = padded * nw
    hbm = pl.BlockSpec(memory_space=pltpu.HBM)
    operands = (x, fir_taps.reshape(1, TAPS), bands, station_live.reshape(1, ns))
    order = np.zeros((nw * groups, -(-ch // 128) * 128), np.float32)
    for w in range(nw):
        for i in range(groups):
            order[w * groups + i, i * nw + w] = 1.0
    operands += spectra_constants() + (order.astype(bf16),)
    return pl.pallas_call(
        spectra_kernel,
        out_shape=jax.ShapeDtypeStruct((2, nw * groups, KEPT), bf16),
        in_specs=[hbm] * len(operands),
        out_specs=pl.BlockSpec(memory_space=pltpu.VMEM),
        scratch_shapes=[pltpu.VMEM(o.shape, o.dtype) for o in operands]
        + [
            pltpu.VMEM((RADIX * ch, 2 * INNER), bf16),
            pltpu.VMEM((2 * NBANDS * ch, BINS), bf16),
            pltpu.SemaphoreType.DMA((len(operands) - 1 + PIECES,)),
        ],
        compiler_params=pltpu.CompilerParams(vmem_limit_bytes=62 * 2**20),
        cost_estimate=pl.CostEstimate(
            flops=3 * 10**9, bytes_accessed=5 * 2**20, transcendentals=0
        ),
        name="spectra",
    )(*operands)


def prepare_kernel(peers, bands_ref, sent_ref, turned_ref):
    _, nw, groups, group_rows, _ = turned_ref.shape
    repeats = group_rows // peers
    local_rows = groups * repeats
    place = lax.broadcasted_iota(jnp.int32, (1, SLOT), 1)
    residue = RADIX * (place % FOLD) + place // FOLD
    for b in range(NBANDS):
        start = bands_ref[0, b]
        f = start + ((residue - start) & (SLOT - 1))
        phase = f.astype(f32) * (math.pi / NT)
        c, sn = jnp.cos(phase), jnp.sin(phase)
        where = slice(b * SLOT, (b + 1) * SLOT)
        re, im = sent_ref[0, :, where].astype(f32), sent_ref[1, :, where].astype(f32)
        for k, value in enumerate((re * c + im * sn, im * c - re * sn)):
            for w in range(nw):
                for group in range(groups):
                    rows = []
                    for i in range(group * repeats, (group + 1) * repeats):
                        at = w * local_rows + i
                        rows.append(jnp.broadcast_to(value[at : at + 1], (peers, SLOT)))
                    turned_ref[k, w, group, :, where] = jnp.concatenate(rows, axis=0).astype(bf16)


def prepare(bands, sent, rows, nw):
    peers = 2 * rows
    fit = [n for n in range(1, rows + 1) if rows % n == 0 and n * peers % 16 == 0]
    repeats = fit[0] if fit else rows
    turned = (2, nw, rows // repeats, repeats * peers, KEPT)
    smem = pl.BlockSpec(memory_space=pltpu.SMEM)
    vmem = pl.BlockSpec(memory_space=pltpu.VMEM)
    return pl.pallas_call(
        functools.partial(prepare_kernel, peers),
        out_shape=jax.ShapeDtypeStruct(turned, bf16),
        in_specs=[smem, vmem],
        out_specs=vmem,
        compiler_params=pltpu.CompilerParams(vmem_limit_bytes=16 * 2**20),
        cost_estimate=pl.CostEstimate(flops=10**7, bytes_accessed=4 * 2**20, transcendentals=0),
        name="prepare",
    )(bands, sent)


def lag_kernel(bands_ref, base_ref, shift_ref, even_ref, odd_ref):
    place = lax.broadcasted_iota(jnp.int32, (SLOT, 1), 0)
    residue = RADIX * (place % FOLD) + place // FOLD
    for b in range(NBANDS):
        start = bands_ref[0, b]
        block = start // SLOT
        first = residue >= start % SLOT
        rows = [
            [shift_ref[k, pl.ds(block + step, 1), :] for step in range(2)] for k in range(2)
        ]
        c = jnp.where(first, rows[0][0], rows[0][1])
        s = jnp.where(first, rows[1][0], rows[1][1])
        weight = jnp.where(first & (residue + block * SLOT == 0), 0.5, 1.0)
        bc, bs = base_ref[0] * weight, base_ref[1] * weight
        even_ref[b * SLOT : (b + 1) * SLOT, :] = (bc * c - bs * s).astype(bf16)
        odd_ref[b * SLOT : (b + 1) * SLOT, :] = (bs * c + bc * s).astype(bf16)


def lag_tables(bands):
    base, shift = lag_constants()
    table = jax.ShapeDtypeStruct((KEPT, HALF), bf16)
    smem = pl.BlockSpec(memory_space=pltpu.SMEM)
    vmem = pl.BlockSpec(memory_space=pltpu.VMEM)
    return pl.pallas_call(
        lag_kernel,
        out_shape=[table, table],
        in_specs=[smem, vmem, vmem],
        out_specs=[vmem, vmem],
        compiler_params=pltpu.CompilerParams(vmem_limit_bytes=16 * 2**20),
        cost_estimate=pl.CostEstimate(flops=10**7, bytes_accessed=4 * 2**20, transcendentals=0),
        name="lag_tables",
    )(bands, base, shift)


def crossed(nw, rows, live, lanes, turned_ref, near_ref, swap_ref, cross_re, cross_im):
    _, _, groups, group_rows, _ = turned_ref.shape
    even_core = lax.rem(lax.axis_index("sta"), 2) == 0
    remote = []
    for k in range(2):
        near, swap = near_ref[k, :, lanes], swap_ref[k, :, lanes]
        by_core = [
            jnp.where(even_core, near, swap).astype(f32) * live,
            jnp.where(even_core, swap, near).astype(f32) * live,
        ]
        remote.append([])
        for w in range(nw):
            span = slice(w * rows, (w + 1) * rows)
            peers = jnp.concatenate([made[span] for made in by_core], axis=0)
            repeats = group_rows // (2 * rows)
            remote[k].append(jnp.concatenate([peers] * repeats, axis=0).astype(bf16))
    for row in range(0, group_rows, 16):
        end = min(row + 16, group_rows)
        there = [
            [remote[k][w][row:end] for w in range(nw)]
            for k in range(2)
        ]
        for group in range(groups):
            re, im = [], []
            for w in range(nw):
                lr = turned_ref[0, w, group, row:end, lanes]
                li = turned_ref[1, w, group, row:end, lanes]
                rr, ri = there[0][w], there[1][w]
                re.append(lr * rr + li * ri)
                im.append(li * rr - lr * ri)
            at = slice(group * group_rows + row, group * group_rows + end)
            cross_re[at, lanes] = (re[0] + re[1]) + (re[2] + re[3])
            cross_im[at, lanes] = (im[0] + im[1]) + (im[2] + im[3])


def mirrored(i, columns, even, odd, value_ref):
    peers, width = even.shape
    backward = 127 - lax.broadcasted_iota(jnp.int32, (peers, 128), 1)
    for tile in range(0, width, 128):
        e, o = even[:, tile : tile + 128], odd[:, tile : tile + 128]
        after = HALF + columns + tile
        before = HALF - columns - tile - 128
        value_ref[i, :, after : after + 128] = e - o
        value_ref[i, :, before : before + 128] = jnp.take_along_axis(e + o, backward, axis=1)


def started(lanes, value_ref, out_ref, block, distance, sem):
    _, chips, _, _, _ = out_ref.shape
    chip = lax.rem(lax.axis_index("sta") // 2 + chips - distance, chips)
    copy = pltpu.make_async_copy(
        value_ref.at[:, :, lanes], out_ref.at[:, chip, :, block, lanes], sem
    )
    copy.start()
    return copy


def correlate_kernel(nw, units, aliased, live_ref, turned_ref, even_ref, odd_ref, *rest):
    sources, rest = rest[: 2 * len(units)], rest[2 * len(units) :]
    if aliased:
        rest = rest[1:]
    out_ref, cross_re, cross_im, values, sems = rest
    rows = out_ref.shape[0]
    total = turned_ref.shape[2] * turned_ref.shape[3]
    peers = total // rows
    bands = [slice(band * SLOT, (band + 1) * SLOT) for band in range(NBANDS)]
    copies = []

    def cross(at, band):
        crossed(
            nw,
            rows,
            live_ref[:, units[at][0] : units[at][0] + 1].astype(f32),
            bands[band],
            turned_ref,
            *sources[2 * at : 2 * at + 2],
            cross_re.at[at],
            cross_im.at[at],
        )

    width = HALF // 2

    def finished(at, step):
        block, distance = units[at]
        columns = step * width
        some = slice(columns, columns + width)
        even = jnp.dot(cross_re[at], even_ref[:, some], preferred_element_type=f32)
        odd = jnp.dot(cross_im[at], odd_ref[:, some], preferred_element_type=f32)
        for i in range(rows):
            span = slice(i * peers, (i + 1) * peers)
            mirrored(i, columns, even[span], odd[span], values.at[at])
        if step == 0:
            made = [pl.ds(HALF - width, 2 * width)]
        else:
            made = [pl.ds(0, HALF - width), pl.ds(HALF + width, HALF - width)]
        for n, lanes in enumerate(made):
            sem = sems.at[at, step + n]
            copies.append(started(lanes, values.at[at], out_ref, block, distance, sem))

    for at in range(len(units) + 1):
        for step in range(2):
            if at < len(units):
                for band in range(step * NBANDS // 2, (step + 1) * NBANDS // 2):
                    cross(at, band)
            if at:
                finished(at - 1, step)
    for copy in copies:
        copy.wait()


def correlate(block_live, turned, tables, rows, chips, units, sources, more=()):
    _, nw, groups, group_rows, _ = turned.shape
    total = groups * group_rows
    peers = 2 * rows
    n = len(units)
    vmem = pl.BlockSpec(memory_space=pltpu.VMEM)
    output = pl.BlockSpec(memory_space=pl.ANY)
    operands = [block_live, turned, *tables, *sources]
    cross = pltpu.VMEM((n, total, KEPT), bf16)
    return pl.pallas_call(
        functools.partial(correlate_kernel, nw, units, bool(more)),
        out_shape=jax.ShapeDtypeStruct((rows, chips, peers, OFFS, LAGS), f32),
        in_specs=[vmem] * len(operands) + [output] * len(more),
        out_specs=output,
        scratch_shapes=[
            cross,
            cross,
            pltpu.VMEM((n, rows, peers, LAGS), f32),
            pltpu.SemaphoreType.DMA((n, 3)),
        ],
        input_output_aliases={len(operands): 0} if more else {},
        compiler_params=pltpu.CompilerParams(vmem_limit_bytes=(24 if more else 32) * 2**20),
        cost_estimate=pl.CostEstimate(
            flops=4 * n * total * KEPT * HALF,
            bytes_accessed=8 * 2**20,
            transcendentals=0,
        ),
        name="block_rows",
    )(*operands, *more)


def next_group(block):
    axes = ("section", "grp")
    n = lax.axis_size(axes)
    return lax.ppermute(block, axes, [((i - 1) % n, i) for i in range(n)])


def swapped_core(block):
    n = lax.axis_size("sta")
    return lax.ppermute(block, "sta", [(i, i ^ 1) for i in range(n)])


def from_chip(block, distance):
    n = lax.axis_size("sta")
    return lax.ppermute(block, "sta", [(i, (i + 2 * distance) % n) for i in range(n)])


def tied(*values):
    return lax.optimization_barrier(values)


def body(records, fir_taps, band_bins, station_live, block_live):
    chips = lax.axis_size("sta") // 2
    ns, nw, nc, _ = records.shape
    rows = ns * nc
    bands = jnp.transpose(band_bins)
    sent = spectra(records, fir_taps, bands, station_live)
    turned = prepare(bands, sent, rows, nw)
    tables = lag_tables(bands)
    first, turned, *tables = tied(next_group(sent), turned, *tables)
    second = next_group(first)
    far = [from_chip(first, d) for d in range(1, chips)]
    near_swap = swapped_core(first)
    far, second = tied(far, second)
    held = [first, near_swap]
    for block in far:
        held += [block, swapped_core(block)]
    far_second = [from_chip(second, d) for d in range(1, chips)]
    near_swap = swapped_core(second)
    live = block_live.reshape(1, OFFS)

    def written(units, held, *more):
        return correlate(live, turned, tables, rows, chips, units, held, more)

    units = [(0, d) for d in range(chips)] + [(1, 0)]
    result = written(units, held + [second, near_swap])
    far_second, result = tied(far_second, result)
    for d in range(1, chips):
        far = far_second[d - 1]
        result = written([(1, d)], [far, swapped_core(far)], result)
    return result.reshape(-1, OFFS, LAGS)


def solution(mesh):
    in_specs = (
        P(("section", "grp", "sta"), None, None, None),
        P(),
        P(),
        P(("section", "grp", "sta")),
        P(("section", "grp")),
    )
    out_specs = P("sta", ("section", "grp"), None)
    return jax.shard_map(body, mesh=mesh, in_specs=in_specs, out_specs=out_specs, check_vma=False)
```

```python
import functools
import math

import jax
import jax.numpy as jnp
import numpy as np
from jax import lax
from jax.experimental import pallas as pl
from jax.experimental.pallas import tpu as pltpu
from jax.sharding import PartitionSpec as P

BINS = 2048
NT = 4096
DEC = 4
RAW = 16384
TAPS = 64
NBANDS = 4
SLOT = 256
OFFS = 2
LAGS = 1024
HALF = LAGS // 2
RADIX = 16
INNER = NT // RADIX
BIG = BINS // RADIX
FOLD = 256 // RADIX
FRAME = 128
SPAN = DEC * FRAME
LEAD = 256
WINDOW = SPAN + LEAD
PIECES = 2
BLOCKS_IN = NT // FRAME
KEPT = NBANDS * SLOT
EPS = 1e-06

f32 = jnp.float32
bf16 = jnp.bfloat16


def by_tile(table):
    padded = np.pad(table, ((0, 0), (0, -table.shape[1] % 128)))
    return np.ascontiguousarray(
        padded.reshape(table.shape[0], -1, 128).transpose(1, 0, 2)
    )


def joined(ref):
    return jnp.concatenate([ref[i] for i in range(ref.shape[0])], axis=1)


def compact_order():
    place = np.arange(SLOT)
    return RADIX * (place % FOLD) + place // FOLD


def spectra_constants():
    inner = np.arange(INNER)
    g = np.arange(BIG)
    angle = 2.0 * np.pi * ((inner[:, None] * g[None, :]) % INNER) / INNER
    cos, sin = np.cos(angle), np.sin(angle)
    table = np.concatenate(
        [np.concatenate([cos, -sin], axis=1), np.concatenate([sin, cos], axis=1)], axis=0
    )
    h = np.arange(RADIX)
    turn = 2.0 * np.pi * (h[:, None] * inner[None, :]) / NT
    twiddle = np.stack([np.cos(turn), -np.sin(turn)]).astype(np.float32)
    fold = np.zeros((RADIX, BIG, SLOT), np.float32)
    for step in range(RADIX):
        fold[step, np.arange(BIG), FOLD * step + np.arange(BIG) % FOLD] = 1.0
    fold = by_tile(fold.reshape(BINS, SLOT).astype(bf16))
    return by_tile(table.astype(np.float32).astype(bf16)), twiddle, fold


def lag_constants():
    q = compact_order()[:, None].astype(np.float64)
    n = np.arange(HALF)[None, :] + 0.5
    angle = 2.0 * np.pi * ((q * 2 * n) % (2 * NT)) / (2 * NT)
    base = np.stack([np.cos(angle), np.sin(angle)]) / math.sqrt(BINS)
    block = np.arange(16)[:, None].astype(np.float64)
    turn = 2.0 * np.pi * ((block * SLOT * 2 * n) % (2 * NT)) / (2 * NT)
    shift = np.stack([np.cos(turn), np.sin(turn)])
    return base.astype(np.float32), shift.astype(np.float32)


def real_dft8(d):
    r = math.sqrt(0.5)
    s = [d[b] + d[b + 4] for b in range(4)]
    t = [d[b] - d[b + 4] for b in range(4)]
    s02, s13 = s[0] + s[2], s[1] + s[3]
    t13m, t13p = r * (t[1] - t[3]), r * (t[1] + t[3])
    return [
        (s02 + s13, None),
        (t[0] + t13m, -(t[2] + t13p)),
        (s[0] - s[2], s[3] - s[1]),
        (t[0] - t13m, t[2] - t13p),
        (s02 - s13, None),
    ]


def real_dft16(d):
    even, odd = real_dft8(d[0::2]), real_dft8(d[1::2])
    y = [None] * 16
    y[0] = (even[0][0] + odd[0][0], None)
    y[8] = (even[0][0] - odd[0][0], None)
    y[4] = (even[4][0], -odd[4][0])
    for h in range(1, 4):
        c, s = math.cos(math.pi * h / 8), -math.sin(math.pi * h / 8)
        re, im = odd[h]
        tr, ti = re * c - im * s, re * s + im * c
        y[h] = (even[h][0] + tr, even[h][1] + ti)
        y[8 - h] = (even[h][0] - tr, ti - even[h][1])
    for h in range(9, 16):
        y[h] = (y[16 - h][0], -y[16 - h][1])
    return y


def spectra_kernel(
    x_hbm,
    taps_hbm,
    bands_hbm,
    live_hbm,
    table_hbm,
    twiddle_hbm,
    fold_hbm,
    order_hbm,
    sent_ref,
    x_ref,
    taps_ref,
    bands_ref,
    live_ref,
    table_ref,
    twiddle_ref,
    fold_ref,
    order_ref,
    turned,
    kept,
    sems,
):
    ch = x_ref.shape[0] * x_ref.shape[1]
    piece = RAW // PIECES
    pairs = [(taps_hbm, taps_ref)]
    for i in range(PIECES):
        lanes = slice(i * piece, (i + 1) * piece)
        pairs.append((x_hbm.at[:, :, lanes], x_ref.at[:, :, lanes]))
    pairs += [
        (twiddle_hbm, twiddle_ref),
        (table_hbm, table_ref),
        (bands_hbm, bands_ref),
        (live_hbm, live_ref),
        (fold_hbm, fold_ref),
        (order_hbm, order_ref),
    ]
    copies = [pltpu.make_async_copy(a, b, sems.at[i]) for i, (a, b) in enumerate(pairs)]
    for copy in copies:
        copy.start()
    tap = lax.broadcasted_iota(jnp.int32, (TAPS, WINDOW), 0)
    place = (lax.broadcasted_iota(jnp.int32, (TAPS, WINDOW), 1) == LEAD - tap).astype(bf16)
    copies[0].wait()
    taps = taps_ref[...]
    taps_high = taps.astype(bf16)
    taps_low = (taps - taps_high.astype(f32)).astype(bf16)

    parts = jnp.concatenate([taps_high, taps_low], axis=0)
    placed = jnp.dot(parts, place, preferred_element_type=f32)

    def toeplitz(row):
        return pltpu.roll(
            jnp.broadcast_to(row, (FRAME, WINDOW)), 0, 1, stride=DEC, stride_axis=0
        ).astype(bf16)

    weights = jnp.concatenate([toeplitz(placed[:1]), toeplitz(placed[1:])], axis=0)
    decimated = []
    tail = jnp.zeros((ch, LEAD), bf16)
    for i in range(PIECES):
        copies[1 + i].wait()
        x = x_ref[:, :, i * piece : (i + 1) * piece].reshape(ch, piece)
        x = jnp.concatenate([tail, x], axis=1)
        tail = x[:, piece:]
        windows = [x[:, at : at + WINDOW] for at in range(0, piece, SPAN)]
        both = lax.dot_general(
            jnp.concatenate(windows, axis=0),
            weights,
            (((1,), (1,)), ((), ())),
            preferred_element_type=f32,
        )
        decimated.append((both[:, :FRAME] + both[:, FRAME:]).astype(bf16).astype(f32))
    each = BLOCKS_IN // PIECES
    copies[1 + PIECES].wait()
    for at in range(0, ch, 16):
        d = []
        for b in range(RADIX):
            pair = []
            for frame in (2 * b, 2 * b + 1):
                row = frame % each * ch + at
                pair.append(decimated[frame // each][row : row + 16])
            d.append(jnp.concatenate(pair, axis=1))
        y = real_dft16(d)
        for h in range(RADIX):
            c = twiddle_ref[0, h : h + 1, :]
            sn = twiddle_ref[1, h : h + 1, :]
            yr, yi = y[h]
            if yi is None:
                ur, ui = yr * c, yr * sn
            else:
                ur, ui = yr * c - yi * sn, yr * sn + yi * c
            for k, u in enumerate((ur, ui)):
                where = slice(k * INNER, (k + 1) * INNER)
                turned[h * ch + at : h * ch + at + 16, where] = u.astype(bf16)

    for copy in copies[2 + PIECES :]:
        copy.wait()
    spectrum = jnp.dot(turned[...], joined(table_ref), preferred_element_type=f32)

    row = lax.broadcasted_iota(jnp.int32, (ch, 1), 0)
    station = row // 12
    live = jnp.zeros((ch, 1), f32)
    station_live = live_ref[...].astype(f32)
    for s_at in range(live_ref.shape[1]):
        live = jnp.where(station == s_at, station_live[:, s_at : s_at + 1], live)
    bands = bands_ref[...]
    edges = [[bands[k : k + 1, b : b + 1] for b in range(NBANDS)] for k in range(2)]

    g = lax.broadcasted_iota(jnp.int32, (1, BIG), 1)
    inside = []
    for h in range(RADIX):
        f = RADIX * g + h
        inside.append(
            [
                ((f >= edges[0][b]) & (f < edges[1][b])).astype(f32)
                for b in range(NBANDS)
            ]
        )
    parts = []
    sums = [jnp.zeros((ch, BIG), f32) for _ in range(NBANDS)]
    for h in range(RADIX):
        re = spectrum[h * ch : (h + 1) * ch, :BIG]
        im = spectrum[h * ch : (h + 1) * ch, BIG:]
        parts.append((re, im))
        power = re * re + im * im
        for b in range(NBANDS):
            sums[b] = sums[b] + power * inside[h][b]
    gains = []
    for b in range(NBANDS):
        width = (edges[1][b] - edges[0][b]).astype(f32)
        energy = jnp.sum(sums[b], axis=1, keepdims=True) / width
        gains.append(lax.rsqrt(energy + EPS) * live)

    for h in range(0, RADIX, 2):
        own = []
        gain = [sum(inside[h + e][b] * gains[b] for b in range(NBANDS)) for e in range(2)]
        for b in range(NBANDS):
            pair = []
            for e in range(2):
                mask = inside[h + e][b]
                for earlier in range(b):
                    mask = mask * (1.0 - inside[h + e][earlier])
                pair.append(mask)
            own.append(jnp.concatenate(pair, axis=1).astype(bf16))
        for k in range(2):
            value = jnp.concatenate([parts[h + e][k] * gain[e] for e in range(2)], axis=1)
            value = value.astype(bf16)
            for b in range(NBANDS):
                at = (2 * b + k) * ch
                kept[at : at + ch, h * BIG : (h + 2) * BIG] = value * own[b]
    compact = jnp.dot(kept[...], joined(fold_ref), preferred_element_type=f32).astype(bf16)
    side = jnp.concatenate([compact[at : at + ch] for at in range(0, 2 * NBANDS * ch, ch)], axis=1)
    order = order_ref[...][:, :ch]
    ordered = jnp.dot(order, side, preferred_element_type=f32).astype(bf16)
    for b in range(NBANDS):
        for k in range(2):
            at = (2 * b + k) * SLOT
            sent_ref[k, :, b * SLOT : (b + 1) * SLOT] = ordered[:, at : at + SLOT]


def spectra(records, fir_taps, bands, station_live):
    ns, nw, nc, _ = records.shape
    x = jnp.transpose(records, (0, 2, 1, 3)).reshape(ns * nc, nw, RAW)
    groups = ns * nc
    padded = -(-groups // 4) * 4
    if padded != groups:
        x = jnp.pad(x, ((0, padded - groups), (0, 0), (0, 0)))
    ch = padded * nw
    hbm = pl.BlockSpec(memory_space=pltpu.HBM)
    operands = (x, fir_taps.reshape(1, TAPS), bands, station_live.reshape(1, ns))
    order = np.zeros((nw * groups, -(-ch // 128) * 128), np.float32)
    for w in range(nw):
        for i in range(groups):
            order[w * groups + i, i * nw + w] = 1.0
    operands += spectra_constants() + (order.astype(bf16),)
    return pl.pallas_call(
        spectra_kernel,
        out_shape=jax.ShapeDtypeStruct((2, nw * groups, KEPT), bf16),
        in_specs=[hbm] * len(operands),
        out_specs=pl.BlockSpec(memory_space=pltpu.VMEM),
        scratch_shapes=[pltpu.VMEM(o.shape, o.dtype) for o in operands]
        + [
            pltpu.VMEM((RADIX * ch, 2 * INNER), bf16),
            pltpu.VMEM((2 * NBANDS * ch, BINS), bf16),
            pltpu.SemaphoreType.DMA((len(operands) - 1 + PIECES,)),
        ],
        compiler_params=pltpu.CompilerParams(vmem_limit_bytes=62 * 2**20),
        cost_estimate=pl.CostEstimate(
            flops=3 * 10**9, bytes_accessed=5 * 2**20, transcendentals=0
        ),
        name="spectra",
    )(*operands)


def prepare_kernel(peers, bands_ref, sent_ref, turned_ref):
    _, nw, groups, group_rows, _ = turned_ref.shape
    repeats = group_rows // peers
    local_rows = groups * repeats
    place = lax.broadcasted_iota(jnp.int32, (1, SLOT), 1)
    residue = RADIX * (place % FOLD) + place // FOLD
    for b in range(NBANDS):
        start = bands_ref[0, b]
        f = start + ((residue - start) & (SLOT - 1))
        phase = f.astype(f32) * (math.pi / NT)
        c, sn = jnp.cos(phase), jnp.sin(phase)
        where = slice(b * SLOT, (b + 1) * SLOT)
        re, im = sent_ref[0, :, where].astype(f32), sent_ref[1, :, where].astype(f32)
        for k, value in enumerate((re * c + im * sn, im * c - re * sn)):
            for w in range(nw):
                for group in range(groups):
                    rows = []
                    for i in range(group * repeats, (group + 1) * repeats):
                        at = w * local_rows + i
                        rows.append(jnp.broadcast_to(value[at : at + 1], (peers, SLOT)))
                    turned_ref[k, w, group, :, where] = jnp.concatenate(rows, axis=0).astype(bf16)


def prepare(bands, sent, rows, nw):
    peers = 2 * rows
    fit = [n for n in range(1, rows + 1) if rows % n == 0 and n * peers % 16 == 0]
    repeats = fit[0] if fit else rows
    turned = (2, nw, rows // repeats, repeats * peers, KEPT)
    smem = pl.BlockSpec(memory_space=pltpu.SMEM)
    vmem = pl.BlockSpec(memory_space=pltpu.VMEM)
    return pl.pallas_call(
        functools.partial(prepare_kernel, peers),
        out_shape=jax.ShapeDtypeStruct(turned, bf16),
        in_specs=[smem, vmem],
        out_specs=vmem,
        compiler_params=pltpu.CompilerParams(vmem_limit_bytes=16 * 2**20),
        cost_estimate=pl.CostEstimate(flops=10**7, bytes_accessed=4 * 2**20, transcendentals=0),
        name="prepare",
    )(bands, sent)


def lag_kernel(bands_ref, base_ref, shift_ref, even_ref, odd_ref):
    place = lax.broadcasted_iota(jnp.int32, (SLOT, 1), 0)
    residue = RADIX * (place % FOLD) + place // FOLD
    for b in range(NBANDS):
        start = bands_ref[0, b]
        block = start // SLOT
        first = residue >= start % SLOT
        rows = [
            [shift_ref[k, pl.ds(block + step, 1), :] for step in range(2)] for k in range(2)
        ]
        c = jnp.where(first, rows[0][0], rows[0][1])
        s = jnp.where(first, rows[1][0], rows[1][1])
        weight = jnp.where(first & (residue + block * SLOT == 0), 0.5, 1.0)
        bc, bs = base_ref[0] * weight, base_ref[1] * weight
        even_ref[b * SLOT : (b + 1) * SLOT, :] = (bc * c - bs * s).astype(bf16)
        odd_ref[b * SLOT : (b + 1) * SLOT, :] = (bs * c + bc * s).astype(bf16)


def lag_tables(bands):
    base, shift = lag_constants()
    table = jax.ShapeDtypeStruct((KEPT, HALF), bf16)
    smem = pl.BlockSpec(memory_space=pltpu.SMEM)
    vmem = pl.BlockSpec(memory_space=pltpu.VMEM)
    return pl.pallas_call(
        lag_kernel,
        out_shape=[table, table],
        in_specs=[smem, vmem, vmem],
        out_specs=[vmem, vmem],
        compiler_params=pltpu.CompilerParams(vmem_limit_bytes=16 * 2**20),
        cost_estimate=pl.CostEstimate(flops=10**7, bytes_accessed=4 * 2**20, transcendentals=0),
        name="lag_tables",
    )(bands, base, shift)


def crossed(nw, rows, live, lanes, turned_ref, near_ref, swap_ref, cross_re, cross_im):
    _, _, groups, group_rows, _ = turned_ref.shape
    even_core = lax.rem(lax.axis_index("sta"), 2) == 0
    remote = []
    for k in range(2):
        near, swap = near_ref[k, :, lanes], swap_ref[k, :, lanes]
        by_core = [
            jnp.where(even_core, near, swap).astype(f32) * live,
            jnp.where(even_core, swap, near).astype(f32) * live,
        ]
        remote.append([])
        for w in range(nw):
            span = slice(w * rows, (w + 1) * rows)
            peers = jnp.concatenate([made[span] for made in by_core], axis=0)
            repeats = group_rows // (2 * rows)
            remote[k].append(jnp.concatenate([peers] * repeats, axis=0).astype(bf16))
    for row in range(0, group_rows, 16):
        end = min(row + 16, group_rows)
        there = [
            [remote[k][w][row:end] for w in range(nw)]
            for k in range(2)
        ]
        for group in range(groups):
            re, im = [], []
            for w in range(nw):
                lr = turned_ref[0, w, group, row:end, lanes]
                li = turned_ref[1, w, group, row:end, lanes]
                rr, ri = there[0][w], there[1][w]
                re.append(lr * rr + li * ri)
                im.append(li * rr - lr * ri)
            at = slice(group * group_rows + row, group * group_rows + end)
            cross_re[at, lanes] = (re[0] + re[1]) + (re[2] + re[3])
            cross_im[at, lanes] = (im[0] + im[1]) + (im[2] + im[3])


def mirrored(i, columns, even, odd, value_ref):
    peers, width = even.shape
    backward = 127 - lax.broadcasted_iota(jnp.int32, (peers, 128), 1)
    for tile in range(0, width, 128):
        e, o = even[:, tile : tile + 128], odd[:, tile : tile + 128]
        after = HALF + columns + tile
        before = HALF - columns - tile - 128
        value_ref[i, :, after : after + 128] = e - o
        value_ref[i, :, before : before + 128] = jnp.take_along_axis(e + o, backward, axis=1)


def started(row, rows, lag, lags, value_ref, out_ref, block, distance, sem):
    _, chips, _, _, _ = out_ref.shape
    chip = lax.rem(lax.axis_index("sta") // 2 + chips - distance, chips)
    mine, lanes = pl.ds(row, rows), pl.ds(lag, lags)
    copy = pltpu.make_async_copy(
        value_ref.at[mine, :, lanes], out_ref.at[mine, chip, :, block, lanes], sem
    )
    copy.start()
    return copy


def correlate_kernel(nw, units, written_by, live_ref, turned_ref, even_ref, odd_ref, *rest):
    sources, rest = rest[: 2 * len(units)], rest[2 * len(units) :]
    keeps, aliased, keeps_in = written_by
    if keeps:
        values, cross_re, cross_im = rest
        values = [values]
    else:
        kept_ref = rest[1] if keeps_in else None
        out_ref, cross_re, cross_im, values, sems = rest[aliased + keeps_in :]
        values = [values.at[at] for at in range(len(units))]
    rows = values[0].shape[0]
    total = turned_ref.shape[2] * turned_ref.shape[3]
    peers = total // rows
    copies = []
    if keeps_in:
        copies.append(started(0, rows, 0, LAGS, kept_ref, out_ref, 1, 0, sems.at[len(units), 0]))
    bands = [slice(band * SLOT, (band + 1) * SLOT) for band in range(NBANDS)]

    def cross(at, band):
        crossed(
            nw,
            rows,
            live_ref[:, units[at][0] : units[at][0] + 1].astype(f32),
            bands[band],
            turned_ref,
            *sources[2 * at : 2 * at + 2],
            cross_re.at[at],
            cross_im.at[at],
        )

    width = HALF // 2

    def finished(at, columns, width):
        block, distance = units[at]
        some = slice(columns, columns + width)
        even = jnp.dot(cross_re[at], even_ref[:, some], preferred_element_type=f32)
        odd = jnp.dot(cross_im[at], odd_ref[:, some], preferred_element_type=f32)
        whole = width == HALF
        for i in range(rows):
            span = slice(i * peers, (i + 1) * peers)
            mirrored(i, columns, even[span], odd[span], values[at])
            if whole:
                copies.append(started(i, 1, 0, LAGS, values[at], out_ref, block, distance, sems.at[at, i]))
        if whole or keeps:
            return
        if columns == 0:
            made = [(HALF - width, 2 * width)]
        else:
            made = [(0, HALF - columns), (HALF + columns, HALF - columns)]
        for n, (first, count) in enumerate(made):
            sem = sems.at[at, columns // width + n]
            copies.append(started(0, rows, first, count, values[at], out_ref, block, distance, sem))

    if len(units) == 1:
        for band in range(NBANDS):
            cross(0, band)
        for step in range(2):
            finished(0, step * width, width)
    else:
        for at in range(len(units) + 1):
            if at < len(units):
                for band in range(NBANDS):
                    cross(at, band)
            if at:
                finished(at - 1, 0, HALF)
    for copy in copies:
        copy.wait()


def correlate(block_live, turned, tables, rows, chips, units, sources, out=(), kept=(), keeps=False):
    _, nw, groups, group_rows, _ = turned.shape
    total = groups * group_rows
    peers = 2 * rows
    n = len(units)
    vmem = pl.BlockSpec(memory_space=pltpu.VMEM)
    output = pl.BlockSpec(memory_space=pl.ANY)
    operands = [block_live, turned, *tables, *sources]
    cross = pltpu.VMEM((n, total, KEPT), bf16)
    value = (rows, peers, LAGS)
    scratch = [cross, cross]
    if not keeps:
        scratch += [
            pltpu.VMEM((n,) + value, f32),
            pltpu.SemaphoreType.DMA((n + 1, max(rows, 3))),
        ]
    shape = value if keeps else (rows, chips, peers, OFFS, LAGS)
    return pl.pallas_call(
        functools.partial(correlate_kernel, nw, units, (keeps, len(out), len(kept))),
        out_shape=jax.ShapeDtypeStruct(shape, f32),
        in_specs=[vmem] * len(operands) + [output] * len(out) + [vmem] * len(kept),
        out_specs=vmem if keeps else output,
        scratch_shapes=scratch,
        input_output_aliases={len(operands): 0} if out else {},
        compiler_params=pltpu.CompilerParams(vmem_limit_bytes=(32 if n > 1 else 24) * 2**20),
        cost_estimate=pl.CostEstimate(
            flops=4 * n * total * KEPT * HALF,
            bytes_accessed=8 * 2**20,
            transcendentals=0,
        ),
        name="kept_rows" if keeps else "block_rows",
    )(*operands, *out, *kept)


def next_group(block):
    axes = ("section", "grp")
    n = lax.axis_size(axes)
    return lax.ppermute(block, axes, [((i - 1) % n, i) for i in range(n)])


def swapped_core(block):
    n = lax.axis_size("sta")
    return lax.ppermute(block, "sta", [(i, i ^ 1) for i in range(n)])


def from_chip(block, distance):
    n = lax.axis_size("sta")
    return lax.ppermute(block, "sta", [(i, (i + 2 * distance) % n) for i in range(n)])


def tied(*values):
    return lax.optimization_barrier(values)


def body(records, fir_taps, band_bins, station_live, block_live):
    chips = lax.axis_size("sta") // 2
    ns, nw, nc, _ = records.shape
    rows = ns * nc
    bands = jnp.transpose(band_bins)
    sent = spectra(records, fir_taps, bands, station_live)
    turned = prepare(bands, sent, rows, nw)
    tables = lag_tables(bands)
    first, turned, *tables = tied(next_group(sent), turned, *tables)
    second = next_group(first)
    far = [from_chip(first, d) for d in range(1, chips)]
    near_swap = swapped_core(first)
    held = [first, near_swap]
    for block in far:
        held += [block, swapped_core(block)]
    held[0], second = tied(held[0], second)
    far_second = [from_chip(second, d) for d in range(1, chips)]
    near_swap = swapped_core(second)
    live = block_live.reshape(1, OFFS)

    def written(units, held, **more):
        return correlate(live, turned, tables, rows, chips, units, held, **more)

    result = written([(0, d) for d in range(chips)], held)
    far_second, result = tied(far_second, result)
    far_swap = [swapped_core(block) for block in far_second]
    near = written([(1, 0)], [second, near_swap], keeps=True)
    far_swap, near = tied(far_swap, near)
    kept = (near,)
    for d in range(1, chips):
        held = [far_second[d - 1], far_swap[d - 1]]
        result = written([(1, d)], held, out=(result,), kept=kept)
        kept = ()
    return result.reshape(-1, OFFS, LAGS)


def solution(mesh):
    in_specs = (
        P(("section", "grp", "sta"), None, None, None),
        P(),
        P(),
        P(("section", "grp", "sta")),
        P(("section", "grp")),
    )
    out_specs = P("sta", ("section", "grp"), None)
    return jax.shard_map(body, mesh=mesh, in_specs=in_specs, out_specs=out_specs, check_vma=False)
```

```python
import functools
import math

import jax
import jax.numpy as jnp
import numpy as np
from jax import lax
from jax.experimental import pallas as pl
from jax.experimental.pallas import tpu as pltpu
from jax.sharding import PartitionSpec as P

BINS = 2048
NT = 4096
DEC = 4
RAW = 16384
TAPS = 64
NBANDS = 4
SLOT = 256
OFFS = 2
LAGS = 1024
HALF = LAGS // 2
RADIX = 16
INNER = NT // RADIX
BIG = BINS // RADIX
FOLD = 256 // RADIX
FRAME = 128
SPAN = DEC * FRAME
LEAD = 256
WINDOW = SPAN + LEAD
PIECES = 2
BLOCKS_IN = NT // FRAME
KEPT = NBANDS * SLOT
EPS = 1e-06

f32 = jnp.float32
bf16 = jnp.bfloat16


def by_tile(table):
    padded = np.pad(table, ((0, 0), (0, -table.shape[1] % 128)))
    return np.ascontiguousarray(
        padded.reshape(table.shape[0], -1, 128).transpose(1, 0, 2)
    )


def joined(ref):
    return jnp.concatenate([ref[i] for i in range(ref.shape[0])], axis=1)


def compact_order():
    place = np.arange(SLOT)
    return RADIX * (place % FOLD) + place // FOLD


def spectra_constants():
    inner = np.arange(INNER)
    g = np.arange(BIG)
    angle = 2.0 * np.pi * ((inner[:, None] * g[None, :]) % INNER) / INNER
    cos, sin = np.cos(angle), np.sin(angle)
    table = np.concatenate(
        [np.concatenate([cos, -sin], axis=1), np.concatenate([sin, cos], axis=1)], axis=0
    )
    h = np.arange(RADIX)
    turn = 2.0 * np.pi * (h[:, None] * inner[None, :]) / NT
    twiddle = np.stack([np.cos(turn), -np.sin(turn)]).astype(np.float32)
    fold = np.zeros((RADIX, BIG, SLOT), np.float32)
    for step in range(RADIX):
        fold[step, np.arange(BIG), FOLD * step + np.arange(BIG) % FOLD] = 1.0
    fold = by_tile(fold.reshape(BINS, SLOT).astype(bf16))
    return by_tile(table.astype(np.float32).astype(bf16)), twiddle, fold


def lag_constants():
    q = compact_order()[:, None].astype(np.float64)
    n = np.arange(HALF)[None, :] + 0.5
    angle = 2.0 * np.pi * ((q * 2 * n) % (2 * NT)) / (2 * NT)
    base = np.stack([np.cos(angle), np.sin(angle)]) / math.sqrt(BINS)
    block = np.arange(16)[:, None].astype(np.float64)
    turn = 2.0 * np.pi * ((block * SLOT * 2 * n) % (2 * NT)) / (2 * NT)
    shift = np.stack([np.cos(turn), np.sin(turn)])
    return base.astype(np.float32), shift.astype(np.float32)


def real_dft8(d):
    r = math.sqrt(0.5)
    s = [d[b] + d[b + 4] for b in range(4)]
    t = [d[b] - d[b + 4] for b in range(4)]
    s02, s13 = s[0] + s[2], s[1] + s[3]
    t13m, t13p = r * (t[1] - t[3]), r * (t[1] + t[3])
    return [
        (s02 + s13, None),
        (t[0] + t13m, -(t[2] + t13p)),
        (s[0] - s[2], s[3] - s[1]),
        (t[0] - t13m, t[2] - t13p),
        (s02 - s13, None),
    ]


def real_dft16(d):
    even, odd = real_dft8(d[0::2]), real_dft8(d[1::2])
    y = [None] * 16
    y[0] = (even[0][0] + odd[0][0], None)
    y[8] = (even[0][0] - odd[0][0], None)
    y[4] = (even[4][0], -odd[4][0])
    for h in range(1, 4):
        c, s = math.cos(math.pi * h / 8), -math.sin(math.pi * h / 8)
        re, im = odd[h]
        tr, ti = re * c - im * s, re * s + im * c
        y[h] = (even[h][0] + tr, even[h][1] + ti)
        y[8 - h] = (even[h][0] - tr, ti - even[h][1])
    for h in range(9, 16):
        y[h] = (y[16 - h][0], -y[16 - h][1])
    return y


def spectra_kernel(
    x_hbm,
    taps_hbm,
    bands_hbm,
    live_hbm,
    table_hbm,
    twiddle_hbm,
    fold_hbm,
    order_hbm,
    sent_ref,
    x_ref,
    taps_ref,
    bands_ref,
    live_ref,
    table_ref,
    twiddle_ref,
    fold_ref,
    order_ref,
    turned,
    kept,
    sems,
):
    ch = x_ref.shape[0] * x_ref.shape[1]
    piece = RAW // PIECES
    pairs = [(taps_hbm, taps_ref)]
    for i in range(PIECES):
        lanes = slice(i * piece, (i + 1) * piece)
        pairs.append((x_hbm.at[:, :, lanes], x_ref.at[:, :, lanes]))
    pairs += [
        (twiddle_hbm, twiddle_ref),
        (table_hbm, table_ref),
        (bands_hbm, bands_ref),
        (live_hbm, live_ref),
        (fold_hbm, fold_ref),
        (order_hbm, order_ref),
    ]
    copies = [pltpu.make_async_copy(a, b, sems.at[i]) for i, (a, b) in enumerate(pairs)]
    for copy in copies:
        copy.start()
    tap = lax.broadcasted_iota(jnp.int32, (TAPS, WINDOW), 0)
    place = (lax.broadcasted_iota(jnp.int32, (TAPS, WINDOW), 1) == LEAD - tap).astype(bf16)
    copies[0].wait()
    taps = taps_ref[...]
    taps_high = taps.astype(bf16)
    taps_low = (taps - taps_high.astype(f32)).astype(bf16)

    parts = jnp.concatenate([taps_high, taps_low], axis=0)
    placed = jnp.dot(parts, place, preferred_element_type=f32)

    def toeplitz(row):
        return pltpu.roll(
            jnp.broadcast_to(row, (FRAME, WINDOW)), 0, 1, stride=DEC, stride_axis=0
        ).astype(bf16)

    weights = jnp.concatenate([toeplitz(placed[:1]), toeplitz(placed[1:])], axis=0)
    decimated = []
    tail = jnp.zeros((ch, LEAD), bf16)
    for i in range(PIECES):
        copies[1 + i].wait()
        x = x_ref[:, :, i * piece : (i + 1) * piece].reshape(ch, piece)
        x = jnp.concatenate([tail, x], axis=1)
        tail = x[:, piece:]
        windows = [x[:, at : at + WINDOW] for at in range(0, piece, SPAN)]
        both = lax.dot_general(
            jnp.concatenate(windows, axis=0),
            weights,
            (((1,), (1,)), ((), ())),
            preferred_element_type=f32,
        )
        decimated.append((both[:, :FRAME] + both[:, FRAME:]).astype(bf16).astype(f32))
    each = BLOCKS_IN // PIECES
    copies[1 + PIECES].wait()
    for at in range(0, ch, ch):
        d = []
        for b in range(RADIX):
            pair = []
            for frame in (2 * b, 2 * b + 1):
                row = frame % each * ch + at
                pair.append(decimated[frame // each][row : row + ch])
            d.append(jnp.concatenate(pair, axis=1))
        y = real_dft16(d)
        for h in range(RADIX):
            c = twiddle_ref[0, h : h + 1, :]
            sn = twiddle_ref[1, h : h + 1, :]
            yr, yi = y[h]
            if yi is None:
                ur, ui = yr * c, yr * sn
            else:
                ur, ui = yr * c - yi * sn, yr * sn + yi * c
            for k, u in enumerate((ur, ui)):
                where = slice(k * INNER, (k + 1) * INNER)
                turned[h * ch + at : h * ch + at + ch, where] = u.astype(bf16)

    for copy in copies[2 + PIECES :]:
        copy.wait()
    spectrum = jnp.dot(turned[...], joined(table_ref), preferred_element_type=f32)

    row = lax.broadcasted_iota(jnp.int32, (ch, 1), 0)
    station = row // 12
    live = jnp.zeros((ch, 1), f32)
    station_live = live_ref[...].astype(f32)
    for s_at in range(live_ref.shape[1]):
        live = jnp.where(station == s_at, station_live[:, s_at : s_at + 1], live)
    bands = bands_ref[...]
    edges = [[bands[k : k + 1, b : b + 1] for b in range(NBANDS)] for k in range(2)]

    g = lax.broadcasted_iota(jnp.int32, (1, BIG), 1)
    inside = []
    for h in range(RADIX):
        f = RADIX * g + h
        inside.append(
            [
                ((f >= edges[0][b]) & (f < edges[1][b])).astype(f32)
                for b in range(NBANDS)
            ]
        )
    parts = []
    sums = [jnp.zeros((ch, BIG), f32) for _ in range(NBANDS)]
    for h in range(RADIX):
        re = spectrum[h * ch : (h + 1) * ch, :BIG]
        im = spectrum[h * ch : (h + 1) * ch, BIG:]
        parts.append((re, im))
        power = re * re + im * im
        for b in range(NBANDS):
            sums[b] = sums[b] + power * inside[h][b]
    gains = []
    for b in range(NBANDS):
        width = (edges[1][b] - edges[0][b]).astype(f32)
        energy = jnp.sum(sums[b], axis=1, keepdims=True) / width
        gains.append(lax.rsqrt(energy + EPS) * live)

    for h in range(0, RADIX, 2):
        own = []
        gain = [sum(inside[h + e][b] * gains[b] for b in range(NBANDS)) for e in range(2)]
        for b in range(NBANDS):
            pair = []
            for e in range(2):
                mask = inside[h + e][b]
                for earlier in range(b):
                    mask = mask * (1.0 - inside[h + e][earlier])
                pair.append(mask)
            own.append(jnp.concatenate(pair, axis=1).astype(bf16))
        for k in range(2):
            value = jnp.concatenate([parts[h + e][k] * gain[e] for e in range(2)], axis=1)
            value = value.astype(bf16)
            for b in range(NBANDS):
                at = (2 * b + k) * ch
                kept[at : at + ch, h * BIG : (h + 2) * BIG] = value * own[b]
    compact = jnp.dot(kept[...], joined(fold_ref), preferred_element_type=f32).astype(bf16)
    side = jnp.concatenate([compact[at : at + ch] for at in range(0, 2 * NBANDS * ch, ch)], axis=1)
    order = order_ref[...][:, :ch]
    ordered = jnp.dot(order, side, preferred_element_type=f32).astype(bf16)
    for b in range(NBANDS):
        for k in range(2):
            at = (2 * b + k) * SLOT
            sent_ref[k, :, b * SLOT : (b + 1) * SLOT] = ordered[:, at : at + SLOT]


def spectra(records, fir_taps, bands, station_live):
    ns, nw, nc, _ = records.shape
    x = jnp.transpose(records, (0, 2, 1, 3)).reshape(ns * nc, nw, RAW)
    groups = ns * nc
    padded = -(-groups // 4) * 4
    if padded != groups:
        x = jnp.pad(x, ((0, padded - groups), (0, 0), (0, 0)))
    ch = padded * nw
    hbm = pl.BlockSpec(memory_space=pltpu.HBM)
    operands = (x, fir_taps.reshape(1, TAPS), bands, station_live.reshape(1, ns))
    order = np.zeros((nw * groups, -(-ch // 128) * 128), np.float32)
    for w in range(nw):
        for i in range(groups):
            order[w * groups + i, i * nw + w] = 1.0
    operands += spectra_constants() + (order.astype(bf16),)
    return pl.pallas_call(
        spectra_kernel,
        out_shape=jax.ShapeDtypeStruct((2, nw * groups, KEPT), bf16),
        in_specs=[hbm] * len(operands),
        out_specs=pl.BlockSpec(memory_space=pltpu.VMEM),
        scratch_shapes=[pltpu.VMEM(o.shape, o.dtype) for o in operands]
        + [
            pltpu.VMEM((RADIX * ch, 2 * INNER), bf16),
            pltpu.VMEM((2 * NBANDS * ch, BINS), bf16),
            pltpu.SemaphoreType.DMA((len(operands) - 1 + PIECES,)),
        ],
        compiler_params=pltpu.CompilerParams(vmem_limit_bytes=62 * 2**20),
        cost_estimate=pl.CostEstimate(
            flops=3 * 10**9, bytes_accessed=5 * 2**20, transcendentals=0
        ),
        name="spectra",
    )(*operands)


def prepare_kernel(peers, bands_ref, sent_ref, turned_ref):
    _, nw, groups, group_rows, _ = turned_ref.shape
    repeats = group_rows // peers
    local_rows = groups * repeats
    place = lax.broadcasted_iota(jnp.int32, (1, SLOT), 1)
    residue = RADIX * (place % FOLD) + place // FOLD
    for b in range(NBANDS):
        start = bands_ref[0, b]
        f = start + ((residue - start) & (SLOT - 1))
        phase = f.astype(f32) * (math.pi / NT)
        c, sn = jnp.cos(phase), jnp.sin(phase)
        where = slice(b * SLOT, (b + 1) * SLOT)
        re, im = sent_ref[0, :, where].astype(f32), sent_ref[1, :, where].astype(f32)
        for k, value in enumerate((re * c + im * sn, im * c - re * sn)):
            for w in range(nw):
                for group in range(groups):
                    rows = []
                    for i in range(group * repeats, (group + 1) * repeats):
                        at = w * local_rows + i
                        rows.append(jnp.broadcast_to(value[at : at + 1], (peers, SLOT)))
                    turned_ref[k, w, group, :, where] = jnp.concatenate(rows, axis=0).astype(bf16)


def prepare(bands, sent, rows, nw):
    peers = 2 * rows
    fit = [n for n in range(1, rows + 1) if rows % n == 0 and n * peers % 16 == 0]
    repeats = fit[0] if fit else rows
    turned = (2, nw, rows // repeats, repeats * peers, KEPT)
    smem = pl.BlockSpec(memory_space=pltpu.SMEM)
    vmem = pl.BlockSpec(memory_space=pltpu.VMEM)
    return pl.pallas_call(
        functools.partial(prepare_kernel, peers),
        out_shape=jax.ShapeDtypeStruct(turned, bf16),
        in_specs=[smem, vmem],
        out_specs=vmem,
        compiler_params=pltpu.CompilerParams(vmem_limit_bytes=16 * 2**20),
        cost_estimate=pl.CostEstimate(flops=10**7, bytes_accessed=4 * 2**20, transcendentals=0),
        name="prepare",
    )(bands, sent)


def lag_kernel(bands_ref, base_ref, shift_ref, even_ref, odd_ref):
    place = lax.broadcasted_iota(jnp.int32, (SLOT, 1), 0)
    residue = RADIX * (place % FOLD) + place // FOLD
    for b in range(NBANDS):
        start = bands_ref[0, b]
        block = start // SLOT
        first = residue >= start % SLOT
        rows = [
            [shift_ref[k, pl.ds(block + step, 1), :] for step in range(2)] for k in range(2)
        ]
        c = jnp.where(first, rows[0][0], rows[0][1])
        s = jnp.where(first, rows[1][0], rows[1][1])
        weight = jnp.where(first & (residue + block * SLOT == 0), 0.5, 1.0)
        bc, bs = base_ref[0] * weight, base_ref[1] * weight
        even_ref[b * SLOT : (b + 1) * SLOT, :] = (bc * c - bs * s).astype(bf16)
        odd_ref[b * SLOT : (b + 1) * SLOT, :] = (bs * c + bc * s).astype(bf16)


def lag_tables(bands):
    base, shift = lag_constants()
    table = jax.ShapeDtypeStruct((KEPT, HALF), bf16)
    smem = pl.BlockSpec(memory_space=pltpu.SMEM)
    vmem = pl.BlockSpec(memory_space=pltpu.VMEM)
    return pl.pallas_call(
        lag_kernel,
        out_shape=[table, table],
        in_specs=[smem, vmem, vmem],
        out_specs=[vmem, vmem],
        compiler_params=pltpu.CompilerParams(vmem_limit_bytes=16 * 2**20),
        cost_estimate=pl.CostEstimate(flops=10**7, bytes_accessed=4 * 2**20, transcendentals=0),
        name="lag_tables",
    )(bands, base, shift)


def crossed(nw, rows, live, lanes, turned_ref, near_ref, swap_ref, cross_re, cross_im):
    _, _, groups, group_rows, _ = turned_ref.shape
    even_core = lax.rem(lax.axis_index("sta"), 2) == 0
    remote = []
    for k in range(2):
        near, swap = near_ref[k, :, lanes], swap_ref[k, :, lanes]
        by_core = [
            jnp.where(even_core, near, swap).astype(f32) * live,
            jnp.where(even_core, swap, near).astype(f32) * live,
        ]
        remote.append([])
        for w in range(nw):
            span = slice(w * rows, (w + 1) * rows)
            peers = jnp.concatenate([made[span] for made in by_core], axis=0)
            repeats = group_rows // (2 * rows)
            remote[k].append(jnp.concatenate([peers] * repeats, axis=0).astype(bf16))
    for row in range(0, group_rows, 16):
        end = min(row + 16, group_rows)
        there = [
            [remote[k][w][row:end] for w in range(nw)]
            for k in range(2)
        ]
        for group in range(groups):
            re, im = [], []
            for w in range(nw):
                lr = turned_ref[0, w, group, row:end, lanes]
                li = turned_ref[1, w, group, row:end, lanes]
                rr, ri = there[0][w], there[1][w]
                re.append(lr * rr + li * ri)
                im.append(li * rr - lr * ri)
            at = slice(group * group_rows + row, group * group_rows + end)
            cross_re[at, lanes] = (re[0] + re[1]) + (re[2] + re[3])
            cross_im[at, lanes] = (im[0] + im[1]) + (im[2] + im[3])


def mirrored(i, columns, even, odd, value_ref):
    peers, width = even.shape
    backward = 127 - lax.broadcasted_iota(jnp.int32, (peers, 128), 1)
    for tile in range(0, width, 128):
        e, o = even[:, tile : tile + 128], odd[:, tile : tile + 128]
        after = HALF + columns + tile
        before = HALF - columns - tile - 128
        value_ref[i, :, after : after + 128] = e - o
        value_ref[i, :, before : before + 128] = jnp.take_along_axis(e + o, backward, axis=1)


def started(row, rows, lag, lags, value_ref, out_ref, block, distance, sem):
    _, chips, _, _, _ = out_ref.shape
    chip = lax.rem(lax.axis_index("sta") // 2 + chips - distance, chips)
    mine, lanes = pl.ds(row, rows), pl.ds(lag, lags)
    copy = pltpu.make_async_copy(
        value_ref.at[mine, :, lanes], out_ref.at[mine, chip, :, block, lanes], sem
    )
    copy.start()
    return copy


def correlate_kernel(nw, units, written_by, live_ref, turned_ref, even_ref, odd_ref, *rest):
    sources, rest = rest[: 2 * len(units)], rest[2 * len(units) :]
    keeps, aliased, keeps_in = written_by
    if keeps:
        values, cross_re, cross_im = rest
        values = [values]
    else:
        kept_ref = rest[1] if keeps_in else None
        out_ref, cross_re, cross_im, values, sems = rest[aliased + keeps_in :]
        values = [values.at[at] for at in range(len(units))]
    rows = values[0].shape[0]
    total = turned_ref.shape[2] * turned_ref.shape[3]
    peers = total // rows
    copies = []
    if keeps_in:
        copies.append(started(0, rows, 0, LAGS, kept_ref, out_ref, 1, 0, sems.at[len(units), 0]))
    bands = [slice(band * SLOT, (band + 1) * SLOT) for band in range(NBANDS)]

    def cross(at, band):
        crossed(
            nw,
            rows,
            live_ref[:, units[at][0] : units[at][0] + 1].astype(f32),
            bands[band],
            turned_ref,
            *sources[2 * at : 2 * at + 2],
            cross_re.at[at],
            cross_im.at[at],
        )

    width = HALF // 2

    def finished(at, columns, width):
        block, distance = units[at]
        some = slice(columns, columns + width)
        even = jnp.dot(cross_re[at], even_ref[:, some], preferred_element_type=f32)
        odd = jnp.dot(cross_im[at], odd_ref[:, some], preferred_element_type=f32)
        whole = width == HALF
        for i in range(rows):
            span = slice(i * peers, (i + 1) * peers)
            mirrored(i, columns, even[span], odd[span], values[at])
            if whole:
                copies.append(started(i, 1, 0, LAGS, values[at], out_ref, block, distance, sems.at[at, i]))
        if whole or keeps:
            return
        if columns == 0:
            made = [(HALF - width, 2 * width)]
        else:
            made = [(0, HALF - columns), (HALF + columns, HALF - columns)]
        for n, (first, count) in enumerate(made):
            sem = sems.at[at, columns // width + n]
            copies.append(started(0, rows, first, count, values[at], out_ref, block, distance, sem))

    if len(units) == 1:
        for band in range(NBANDS):
            cross(0, band)
        for step in range(2):
            finished(0, step * width, width)
    else:
        for at in range(len(units) + 1):
            if at < len(units):
                for band in range(NBANDS):
                    cross(at, band)
            if at:
                finished(at - 1, 0, HALF)
    for copy in copies:
        copy.wait()


def correlate(block_live, turned, tables, rows, chips, units, sources, out=(), kept=(), keeps=False):
    _, nw, groups, group_rows, _ = turned.shape
    total = groups * group_rows
    peers = 2 * rows
    n = len(units)
    vmem = pl.BlockSpec(memory_space=pltpu.VMEM)
    output = pl.BlockSpec(memory_space=pl.ANY)
    operands = [block_live, turned, *tables, *sources]
    cross = pltpu.VMEM((n, total, KEPT), bf16)
    value = (rows, peers, LAGS)
    scratch = [cross, cross]
    if not keeps:
        scratch += [
            pltpu.VMEM((n,) + value, f32),
            pltpu.SemaphoreType.DMA((n + 1, max(rows, 3))),
        ]
    shape = value if keeps else (rows, chips, peers, OFFS, LAGS)
    return pl.pallas_call(
        functools.partial(correlate_kernel, nw, units, (keeps, len(out), len(kept))),
        out_shape=jax.ShapeDtypeStruct(shape, f32),
        in_specs=[vmem] * len(operands) + [output] * len(out) + [vmem] * len(kept),
        out_specs=vmem if keeps else output,
        scratch_shapes=scratch,
        input_output_aliases={len(operands): 0} if out else {},
        compiler_params=pltpu.CompilerParams(vmem_limit_bytes=(32 if n > 1 else 24) * 2**20),
        cost_estimate=pl.CostEstimate(
            flops=4 * n * total * KEPT * HALF,
            bytes_accessed=8 * 2**20,
            transcendentals=0,
        ),
        name="kept_rows" if keeps else "block_rows",
    )(*operands, *out, *kept)


def next_group(block):
    axes = ("section", "grp")
    n = lax.axis_size(axes)
    return lax.ppermute(block, axes, [((i - 1) % n, i) for i in range(n)])


def swapped_core(block):
    n = lax.axis_size("sta")
    return lax.ppermute(block, "sta", [(i, i ^ 1) for i in range(n)])


def from_chip(block, distance):
    n = lax.axis_size("sta")
    return lax.ppermute(block, "sta", [(i, (i + 2 * distance) % n) for i in range(n)])


def tied(*values):
    return lax.optimization_barrier(values)


def body(records, fir_taps, band_bins, station_live, block_live):
    chips = lax.axis_size("sta") // 2
    ns, nw, nc, _ = records.shape
    rows = ns * nc
    bands = jnp.transpose(band_bins)
    sent = spectra(records, fir_taps, bands, station_live)
    turned = prepare(bands, sent, rows, nw)
    tables = lag_tables(bands)
    first, turned, *tables = tied(next_group(sent), turned, *tables)
    second = next_group(first)
    far = [from_chip(first, d) for d in range(1, chips)]
    near_swap = swapped_core(first)
    held = [first, near_swap]
    for block in far:
        held += [block, swapped_core(block)]
    held[0], second = tied(held[0], second)
    far_second = [from_chip(second, d) for d in range(1, chips)]
    near_swap = swapped_core(second)
    live = block_live.reshape(1, OFFS)

    def written(units, held, **more):
        return correlate(live, turned, tables, rows, chips, units, held, **more)

    result = written([(0, d) for d in range(chips)], held)
    far_second, result = tied(far_second, result)
    far_swap = [swapped_core(block) for block in far_second]
    near = written([(1, 0)], [second, near_swap], keeps=True)
    far_swap, near = tied(far_swap, near)
    kept = (near,)
    for d in range(1, chips):
        held = [far_second[d - 1], far_swap[d - 1]]
        result = written([(1, d)], held, out=(result,), kept=kept)
        kept = ()
    return result.reshape(-1, OFFS, LAGS)


def solution(mesh):
    in_specs = (
        P(("section", "grp", "sta"), None, None, None),
        P(),
        P(),
        P(("section", "grp", "sta")),
        P(("section", "grp")),
    )
    out_specs = P("sta", ("section", "grp"), None)
    return jax.shard_map(body, mesh=mesh, in_specs=in_specs, out_specs=out_specs, check_vma=False)
```

```python
import functools
import math

import jax
import jax.numpy as jnp
import numpy as np
from jax import lax
from jax.experimental import pallas as pl
from jax.experimental.pallas import tpu as pltpu
from jax.sharding import PartitionSpec as P

BINS = 2048
NT = 4096
DEC = 4
RAW = 16384
TAPS = 64
NBANDS = 4
SLOT = 256
OFFS = 2
LAGS = 1024
HALF = LAGS // 2
RADIX = 16
INNER = NT // RADIX
BIG = BINS // RADIX
FOLD = 256 // RADIX
FRAME = 128
SPAN = DEC * FRAME
LEAD = 256
WINDOW = SPAN + LEAD
PIECES = 2
BLOCKS_IN = NT // FRAME
KEPT = NBANDS * SLOT
EPS = 1e-06

f32 = jnp.float32
bf16 = jnp.bfloat16


def by_tile(table):
    padded = np.pad(table, ((0, 0), (0, -table.shape[1] % 128)))
    return np.ascontiguousarray(
        padded.reshape(table.shape[0], -1, 128).transpose(1, 0, 2)
    )


def joined(ref):
    return jnp.concatenate([ref[i] for i in range(ref.shape[0])], axis=1)


def compact_order():
    place = np.arange(SLOT)
    return RADIX * (place % FOLD) + place // FOLD


def spectra_constants():
    inner = np.arange(INNER)
    g = np.arange(BIG)
    angle = 2.0 * np.pi * ((inner[:, None] * g[None, :]) % INNER) / INNER
    cos, sin = np.cos(angle), np.sin(angle)
    table = np.concatenate(
        [np.concatenate([cos, -sin], axis=1), np.concatenate([sin, cos], axis=1)], axis=0
    )
    h = np.arange(RADIX)
    turn = 2.0 * np.pi * (h[:, None] * inner[None, :]) / NT
    twiddle = np.stack([np.cos(turn), -np.sin(turn)]).astype(np.float32)
    fold = np.zeros((RADIX, BIG, SLOT), np.float32)
    for step in range(RADIX):
        fold[step, np.arange(BIG), FOLD * step + np.arange(BIG) % FOLD] = 1.0
    fold = by_tile(fold.reshape(BINS, SLOT).astype(bf16))
    return by_tile(table.astype(np.float32).astype(bf16)), twiddle, fold


def lag_constants():
    q = compact_order()[:, None].astype(np.float64)
    n = np.arange(HALF)[None, :] + 0.5
    angle = 2.0 * np.pi * ((q * 2 * n) % (2 * NT)) / (2 * NT)
    base = np.stack([np.cos(angle), np.sin(angle)]) / math.sqrt(BINS)
    block = np.arange(16)[:, None].astype(np.float64)
    turn = 2.0 * np.pi * ((block * SLOT * 2 * n) % (2 * NT)) / (2 * NT)
    shift = np.stack([np.cos(turn), np.sin(turn)])
    return base.astype(np.float32), shift.astype(np.float32)


def real_dft8(d):
    r = math.sqrt(0.5)
    s = [d[b] + d[b + 4] for b in range(4)]
    t = [d[b] - d[b + 4] for b in range(4)]
    s02, s13 = s[0] + s[2], s[1] + s[3]
    t13m, t13p = r * (t[1] - t[3]), r * (t[1] + t[3])
    return [
        (s02 + s13, None),
        (t[0] + t13m, -(t[2] + t13p)),
        (s[0] - s[2], s[3] - s[1]),
        (t[0] - t13m, t[2] - t13p),
        (s02 - s13, None),
    ]


def real_dft16(d):
    even, odd = real_dft8(d[0::2]), real_dft8(d[1::2])
    y = [None] * 16
    y[0] = (even[0][0] + odd[0][0], None)
    y[8] = (even[0][0] - odd[0][0], None)
    y[4] = (even[4][0], -odd[4][0])
    for h in range(1, 4):
        c, s = math.cos(math.pi * h / 8), -math.sin(math.pi * h / 8)
        re, im = odd[h]
        tr, ti = re * c - im * s, re * s + im * c
        y[h] = (even[h][0] + tr, even[h][1] + ti)
        y[8 - h] = (even[h][0] - tr, ti - even[h][1])
    for h in range(9, 16):
        y[h] = (y[16 - h][0], -y[16 - h][1])
    return y


def spectra_kernel(
    x_hbm,
    taps_hbm,
    bands_hbm,
    live_hbm,
    table_hbm,
    twiddle_hbm,
    fold_hbm,
    order_hbm,
    sent_ref,
    x_ref,
    taps_ref,
    bands_ref,
    live_ref,
    table_ref,
    twiddle_ref,
    fold_ref,
    order_ref,
    turned,
    kept,
    sems,
):
    ch = x_ref.shape[0] * x_ref.shape[1]
    piece = RAW // PIECES
    pairs = [(taps_hbm, taps_ref)]
    for i in range(PIECES):
        lanes = slice(i * piece, (i + 1) * piece)
        pairs.append((x_hbm.at[:, :, lanes], x_ref.at[:, :, lanes]))
    pairs += [
        (twiddle_hbm, twiddle_ref),
        (table_hbm, table_ref),
        (bands_hbm, bands_ref),
        (live_hbm, live_ref),
        (fold_hbm, fold_ref),
        (order_hbm, order_ref),
    ]
    copies = [pltpu.make_async_copy(a, b, sems.at[i]) for i, (a, b) in enumerate(pairs)]
    for copy in copies:
        copy.start()
    tap = lax.broadcasted_iota(jnp.int32, (TAPS, WINDOW), 0)
    place = (lax.broadcasted_iota(jnp.int32, (TAPS, WINDOW), 1) == LEAD - tap).astype(bf16)
    copies[0].wait()
    taps = taps_ref[...]
    taps_high = taps.astype(bf16)
    taps_low = (taps - taps_high.astype(f32)).astype(bf16)

    parts = jnp.concatenate([taps_high, taps_low], axis=0)
    placed = jnp.dot(parts, place, preferred_element_type=f32)

    def toeplitz(row):
        return pltpu.roll(
            jnp.broadcast_to(row, (FRAME, WINDOW)), 0, 1, stride=DEC, stride_axis=0
        ).astype(bf16)

    weights = jnp.concatenate([toeplitz(placed[:1]), toeplitz(placed[1:])], axis=0)
    decimated = []
    tail = jnp.zeros((ch, LEAD), bf16)
    for i in range(PIECES):
        copies[1 + i].wait()
        x = x_ref[:, :, i * piece : (i + 1) * piece].reshape(ch, piece)
        x = jnp.concatenate([tail, x], axis=1)
        tail = x[:, piece:]
        windows = [x[:, at : at + WINDOW] for at in range(0, piece, SPAN)]
        both = lax.dot_general(
            jnp.concatenate(windows, axis=0),
            weights,
            (((1,), (1,)), ((), ())),
            preferred_element_type=f32,
        )
        decimated.append((both[:, :FRAME] + both[:, FRAME:]).astype(bf16).astype(f32))
    each = BLOCKS_IN // PIECES
    copies[1 + PIECES].wait()
    for at in range(0, ch, 16):
        d = []
        for b in range(RADIX):
            pair = []
            for frame in (2 * b, 2 * b + 1):
                row = frame % each * ch + at
                pair.append(decimated[frame // each][row : row + 16])
            d.append(jnp.concatenate(pair, axis=1))
        y = real_dft16(d)
        for h in range(RADIX):
            c = twiddle_ref[0, h : h + 1, :]
            sn = twiddle_ref[1, h : h + 1, :]
            yr, yi = y[h]
            if yi is None:
                ur, ui = yr * c, yr * sn
            else:
                ur, ui = yr * c - yi * sn, yr * sn + yi * c
            for k, u in enumerate((ur, ui)):
                where = slice(k * INNER, (k + 1) * INNER)
                turned[h * ch + at : h * ch + at + 16, where] = u.astype(bf16)

    for copy in copies[2 + PIECES :]:
        copy.wait()
    spectrum = jnp.dot(turned[...], joined(table_ref), preferred_element_type=f32)

    row = lax.broadcasted_iota(jnp.int32, (ch, 1), 0)
    station = row // 12
    live = jnp.zeros((ch, 1), f32)
    station_live = live_ref[...].astype(f32)
    for s_at in range(live_ref.shape[1]):
        live = jnp.where(station == s_at, station_live[:, s_at : s_at + 1], live)
    bands = bands_ref[...]
    edges = [[bands[k : k + 1, b : b + 1] for b in range(NBANDS)] for k in range(2)]

    g = lax.broadcasted_iota(jnp.int32, (1, BIG), 1)
    inside = []
    for h in range(RADIX):
        f = RADIX * g + h
        inside.append(
            [
                ((f >= edges[0][b]) & (f < edges[1][b])).astype(f32)
                for b in range(NBANDS)
            ]
        )
    parts = []
    sums = [jnp.zeros((ch, BIG), f32) for _ in range(NBANDS)]
    for h in range(RADIX):
        re = spectrum[h * ch : (h + 1) * ch, :BIG]
        im = spectrum[h * ch : (h + 1) * ch, BIG:]
        parts.append((re, im))
        power = re * re + im * im
        for b in range(NBANDS):
            sums[b] = sums[b] + power * inside[h][b]
    gains = []
    for b in range(NBANDS):
        width = (edges[1][b] - edges[0][b]).astype(f32)
        energy = jnp.sum(sums[b], axis=1, keepdims=True) / width
        gains.append(lax.rsqrt(energy + EPS) * live)

    for h in range(0, RADIX, 2):
        own = []
        gain = [sum(inside[h + e][b] * gains[b] for b in range(NBANDS)) for e in range(2)]
        for b in range(NBANDS):
            pair = []
            for e in range(2):
                mask = inside[h + e][b]
                for earlier in range(b):
                    mask = mask * (1.0 - inside[h + e][earlier])
                pair.append(mask)
            own.append(jnp.concatenate(pair, axis=1).astype(bf16))
        for k in range(2):
            value = jnp.concatenate([parts[h + e][k] * gain[e] for e in range(2)], axis=1)
            value = value.astype(bf16)
            for b in range(NBANDS):
                at = (2 * b + k) * ch
                kept[at : at + ch, h * BIG : (h + 2) * BIG] = value * own[b]
    compact = jnp.dot(kept[...], joined(fold_ref), preferred_element_type=f32).astype(bf16)
    side = jnp.concatenate([compact[at : at + ch] for at in range(0, 2 * NBANDS * ch, ch)], axis=1)
    order = order_ref[...][:, :ch]
    ordered = jnp.dot(order, side, preferred_element_type=f32).astype(bf16)
    for b in range(NBANDS):
        for k in range(2):
            at = (2 * b + k) * SLOT
            sent_ref[k, :, b * SLOT : (b + 1) * SLOT] = ordered[:, at : at + SLOT]


def spectra(records, fir_taps, bands, station_live):
    ns, nw, nc, _ = records.shape
    x = jnp.transpose(records, (0, 2, 1, 3)).reshape(ns * nc, nw, RAW)
    groups = ns * nc
    padded = -(-groups // 4) * 4
    if padded != groups:
        x = jnp.pad(x, ((0, padded - groups), (0, 0), (0, 0)))
    ch = padded * nw
    hbm = pl.BlockSpec(memory_space=pltpu.HBM)
    operands = (x, fir_taps.reshape(1, TAPS), bands, station_live.reshape(1, ns))
    order = np.zeros((nw * groups, -(-ch // 128) * 128), np.float32)
    for w in range(nw):
        for i in range(groups):
            order[w * groups + i, i * nw + w] = 1.0
    operands += spectra_constants() + (order.astype(bf16),)
    return pl.pallas_call(
        spectra_kernel,
        out_shape=jax.ShapeDtypeStruct((2, nw * groups, KEPT), bf16),
        in_specs=[hbm] * len(operands),
        out_specs=pl.BlockSpec(memory_space=pltpu.VMEM),
        scratch_shapes=[pltpu.VMEM(o.shape, o.dtype) for o in operands]
        + [
            pltpu.VMEM((RADIX * ch, 2 * INNER), bf16),
            pltpu.VMEM((2 * NBANDS * ch, BINS), bf16),
            pltpu.SemaphoreType.DMA((len(operands) - 1 + PIECES,)),
        ],
        compiler_params=pltpu.CompilerParams(vmem_limit_bytes=62 * 2**20),
        cost_estimate=pl.CostEstimate(
            flops=3 * 10**9, bytes_accessed=5 * 2**20, transcendentals=0
        ),
        name="spectra",
    )(*operands)


def prepare_kernel(peers, bands_ref, sent_ref, turned_ref):
    _, nw, groups, group_rows, _ = turned_ref.shape
    repeats = group_rows // peers
    local_rows = groups * repeats
    place = lax.broadcasted_iota(jnp.int32, (1, SLOT), 1)
    residue = RADIX * (place % FOLD) + place // FOLD
    for b in range(NBANDS):
        start = bands_ref[0, b]
        f = start + ((residue - start) & (SLOT - 1))
        phase = f.astype(f32) * (math.pi / NT)
        c, sn = jnp.cos(phase), jnp.sin(phase)
        where = slice(b * SLOT, (b + 1) * SLOT)
        re, im = sent_ref[0, :, where].astype(f32), sent_ref[1, :, where].astype(f32)
        for k, value in enumerate((re * c + im * sn, im * c - re * sn)):
            for w in range(nw):
                for group in range(groups):
                    rows = []
                    for i in range(group * repeats, (group + 1) * repeats):
                        at = w * local_rows + i
                        rows.append(jnp.broadcast_to(value[at : at + 1], (peers, SLOT)))
                    turned_ref[k, w, group, :, where] = jnp.concatenate(rows, axis=0).astype(bf16)


def prepare(bands, sent, rows, nw):
    peers = 2 * rows
    fit = [n for n in range(1, rows + 1) if rows % n == 0 and n * peers % 16 == 0]
    repeats = fit[0] if fit else rows
    turned = (2, nw, rows // repeats, repeats * peers, KEPT)
    smem = pl.BlockSpec(memory_space=pltpu.SMEM)
    vmem = pl.BlockSpec(memory_space=pltpu.VMEM)
    return pl.pallas_call(
        functools.partial(prepare_kernel, peers),
        out_shape=jax.ShapeDtypeStruct(turned, bf16),
        in_specs=[smem, vmem],
        out_specs=vmem,
        compiler_params=pltpu.CompilerParams(vmem_limit_bytes=16 * 2**20),
        cost_estimate=pl.CostEstimate(flops=10**7, bytes_accessed=4 * 2**20, transcendentals=0),
        name="prepare",
    )(bands, sent)


def lag_kernel(bands_ref, base_ref, shift_ref, even_ref, odd_ref):
    place = lax.broadcasted_iota(jnp.int32, (SLOT, 1), 0)
    residue = RADIX * (place % FOLD) + place // FOLD
    for b in range(NBANDS):
        start = bands_ref[0, b]
        block = start // SLOT
        first = residue >= start % SLOT
        rows = [
            [shift_ref[k, pl.ds(block + step, 1), :] for step in range(2)] for k in range(2)
        ]
        c = jnp.where(first, rows[0][0], rows[0][1])
        s = jnp.where(first, rows[1][0], rows[1][1])
        weight = jnp.where(first & (residue + block * SLOT == 0), 0.5, 1.0)
        bc, bs = base_ref[0] * weight, base_ref[1] * weight
        even_ref[b * SLOT : (b + 1) * SLOT, :] = (bc * c - bs * s).astype(bf16)
        odd_ref[b * SLOT : (b + 1) * SLOT, :] = (bs * c + bc * s).astype(bf16)


def lag_tables(bands):
    base, shift = lag_constants()
    table = jax.ShapeDtypeStruct((KEPT, HALF), bf16)
    smem = pl.BlockSpec(memory_space=pltpu.SMEM)
    vmem = pl.BlockSpec(memory_space=pltpu.VMEM)
    return pl.pallas_call(
        lag_kernel,
        out_shape=[table, table],
        in_specs=[smem, vmem, vmem],
        out_specs=[vmem, vmem],
        compiler_params=pltpu.CompilerParams(vmem_limit_bytes=16 * 2**20),
        cost_estimate=pl.CostEstimate(flops=10**7, bytes_accessed=4 * 2**20, transcendentals=0),
        name="lag_tables",
    )(bands, base, shift)


def crossed(nw, rows, live, lanes, turned_ref, near_ref, swap_ref, cross_re, cross_im):
    _, _, groups, group_rows, _ = turned_ref.shape
    even_core = lax.rem(lax.axis_index("sta"), 2) == 0
    remote = []
    for k in range(2):
        near, swap = near_ref[k, :, lanes], swap_ref[k, :, lanes]
        by_core = [
            jnp.where(even_core, near, swap).astype(f32) * live,
            jnp.where(even_core, swap, near).astype(f32) * live,
        ]
        remote.append([])
        for w in range(nw):
            span = slice(w * rows, (w + 1) * rows)
            peers = jnp.concatenate([made[span] for made in by_core], axis=0)
            repeats = group_rows // (2 * rows)
            remote[k].append(jnp.concatenate([peers] * repeats, axis=0).astype(bf16))
    for row in range(0, group_rows, 16):
        end = min(row + 16, group_rows)
        there = [
            [remote[k][w][row:end] for w in range(nw)]
            for k in range(2)
        ]
        for group in range(groups):
            re, im = [], []
            for w in range(nw):
                lr = turned_ref[0, w, group, row:end, lanes]
                li = turned_ref[1, w, group, row:end, lanes]
                rr, ri = there[0][w], there[1][w]
                re.append(lr * rr + li * ri)
                im.append(li * rr - lr * ri)
            at = slice(group * group_rows + row, group * group_rows + end)
            cross_re[at, lanes] = (re[0] + re[1]) + (re[2] + re[3])
            cross_im[at, lanes] = (im[0] + im[1]) + (im[2] + im[3])


def mirrored(i, columns, even, odd, value_ref):
    peers, width = even.shape
    backward = 127 - lax.broadcasted_iota(jnp.int32, (peers, 128), 1)
    for tile in range(0, width, 128):
        e, o = even[:, tile : tile + 128], odd[:, tile : tile + 128]
        after = HALF + columns + tile
        before = HALF - columns - tile - 128
        value_ref[i, :, after : after + 128] = e - o
        value_ref[i, :, before : before + 128] = jnp.take_along_axis(e + o, backward, axis=1)


def started(row, rows, lag, lags, value_ref, out_ref, block, distance, sem):
    _, chips, _, _, _ = out_ref.shape
    chip = lax.rem(lax.axis_index("sta") // 2 + chips - distance, chips)
    mine, lanes = pl.ds(row, rows), pl.ds(lag, lags)
    copy = pltpu.make_async_copy(
        value_ref.at[mine, :, lanes], out_ref.at[mine, chip, :, block, lanes], sem
    )
    copy.start()
    return copy


def correlate_kernel(nw, units, written_by, live_ref, turned_ref, even_ref, odd_ref, *rest):
    sources, rest = rest[: 2 * len(units)], rest[2 * len(units) :]
    keeps, aliased, keeps_in = written_by
    if keeps:
        values, cross_re, cross_im = rest
        values = [values]
    else:
        kept_ref = rest[1] if keeps_in else None
        out_ref, cross_re, cross_im, values, sems = rest[aliased + keeps_in :]
        values = [values.at[at] for at in range(len(units))]
    rows = values[0].shape[0]
    total = turned_ref.shape[2] * turned_ref.shape[3]
    peers = total // rows
    copies = []
    if keeps_in:
        copies.append(started(0, rows, 0, LAGS, kept_ref, out_ref, 1, 0, sems.at[len(units), 0]))
    bands = [slice(band * SLOT, (band + 1) * SLOT) for band in range(NBANDS)]

    def cross(at, band):
        crossed(
            nw,
            rows,
            live_ref[:, units[at][0] : units[at][0] + 1].astype(f32),
            bands[band],
            turned_ref,
            *sources[2 * at : 2 * at + 2],
            cross_re.at[at],
            cross_im.at[at],
        )

    width = HALF // 2

    def finished(at, columns, width):
        block, distance = units[at]
        some = slice(columns, columns + width)
        even = jnp.dot(cross_re[at], even_ref[:, some], preferred_element_type=f32)
        odd = jnp.dot(cross_im[at], odd_ref[:, some], preferred_element_type=f32)
        whole = width == HALF
        for i in range(rows):
            span = slice(i * peers, (i + 1) * peers)
            mirrored(i, columns, even[span], odd[span], values[at])
            if whole:
                copies.append(started(i, 1, 0, LAGS, values[at], out_ref, block, distance, sems.at[at, i]))
        if whole or keeps:
            return
        if columns == 0:
            made = [(HALF - width, 2 * width)]
        else:
            made = [(0, HALF - columns), (HALF + columns, HALF - columns)]
        for n, (first, count) in enumerate(made):
            sem = sems.at[at, columns // width + n]
            copies.append(started(0, rows, first, count, values[at], out_ref, block, distance, sem))

    if len(units) == 1:
        for band in range(NBANDS):
            cross(0, band)
        for step in range(2):
            finished(0, step * width, width)
    else:
        for at in range(len(units) + 1):
            if at < len(units):
                for band in range(NBANDS):
                    cross(at, band)
            if at == len(units):
                for step in range(2):
                    finished(at - 1, step * width, width)
            elif at:
                finished(at - 1, 0, HALF)
    for copy in copies:
        copy.wait()


def correlate(block_live, turned, tables, rows, chips, units, sources, out=(), kept=(), keeps=False):
    _, nw, groups, group_rows, _ = turned.shape
    total = groups * group_rows
    peers = 2 * rows
    n = len(units)
    vmem = pl.BlockSpec(memory_space=pltpu.VMEM)
    output = pl.BlockSpec(memory_space=pl.ANY)
    operands = [block_live, turned, *tables, *sources]
    cross = pltpu.VMEM((n, total, KEPT), bf16)
    value = (rows, peers, LAGS)
    scratch = [cross, cross]
    if not keeps:
        scratch += [
            pltpu.VMEM((n,) + value, f32),
            pltpu.SemaphoreType.DMA((n + 1, max(rows, 3))),
        ]
    shape = value if keeps else (rows, chips, peers, OFFS, LAGS)
    return pl.pallas_call(
        functools.partial(correlate_kernel, nw, units, (keeps, len(out), len(kept))),
        out_shape=jax.ShapeDtypeStruct(shape, f32),
        in_specs=[vmem] * len(operands) + [output] * len(out) + [vmem] * len(kept),
        out_specs=vmem if keeps else output,
        scratch_shapes=scratch,
        input_output_aliases={len(operands): 0} if out else {},
        compiler_params=pltpu.CompilerParams(vmem_limit_bytes=(32 if n > 1 else 24) * 2**20),
        cost_estimate=pl.CostEstimate(
            flops=4 * n * total * KEPT * HALF,
            bytes_accessed=8 * 2**20,
            transcendentals=0,
        ),
        name="kept_rows" if keeps else "block_rows",
    )(*operands, *out, *kept)


def next_group(block):
    axes = ("section", "grp")
    n = lax.axis_size(axes)
    return lax.ppermute(block, axes, [((i - 1) % n, i) for i in range(n)])


def swapped_core(block):
    n = lax.axis_size("sta")
    return lax.ppermute(block, "sta", [(i, i ^ 1) for i in range(n)])


def from_chip(block, distance):
    n = lax.axis_size("sta")
    return lax.ppermute(block, "sta", [(i, (i + 2 * distance) % n) for i in range(n)])


def tied(*values):
    return lax.optimization_barrier(values)


def body(records, fir_taps, band_bins, station_live, block_live):
    chips = lax.axis_size("sta") // 2
    ns, nw, nc, _ = records.shape
    rows = ns * nc
    bands = jnp.transpose(band_bins)
    sent = spectra(records, fir_taps, bands, station_live)
    turned = prepare(bands, sent, rows, nw)
    tables = lag_tables(bands)
    first, turned, *tables = tied(next_group(sent), turned, *tables)
    second = next_group(first)
    far = [from_chip(first, d) for d in range(1, chips)]
    near_swap = swapped_core(first)
    held = [first, near_swap]
    for block in far:
        held += [block, swapped_core(block)]
    held[0], second = tied(held[0], second)
    far_second = [from_chip(second, d) for d in range(1, chips)]
    near_swap = swapped_core(second)
    live = block_live.reshape(1, OFFS)

    def written(units, held, **more):
        return correlate(live, turned, tables, rows, chips, units, held, **more)

    result = written([(0, d) for d in range(chips)], held)
    far_second, result = tied(far_second, result)
    far_swap = [swapped_core(block) for block in far_second]
    near = written([(1, 0)], [second, near_swap], keeps=True)
    far_swap, near = tied(far_swap, near)
    kept = (near,)
    for d in range(1, chips):
        held = [far_second[d - 1], far_swap[d - 1]]
        result = written([(1, d)], held, out=(result,), kept=kept)
        kept = ()
    return result.reshape(-1, OFFS, LAGS)


def solution(mesh):
    in_specs = (
        P(("section", "grp", "sta"), None, None, None),
        P(),
        P(),
        P(("section", "grp", "sta")),
        P(("section", "grp")),
    )
    out_specs = P("sta", ("section", "grp"), None)
    return jax.shard_map(body, mesh=mesh, in_specs=in_specs, out_specs=out_specs, check_vma=False)
```
